256 devices in a mesh: wide: 64 (over x, z, core), grp: 4 (over y).
Axes of the slice: x: 4, y: 4, z: 8, core: 2. Of those that a mesh axis runs over, the one named last changes fastest.
Arguments:
- inst_rows: bfloat16 [262144, 768], P(('wide', 'grp')), may hold values from -6 to 6
- inst_labels: int32 [262144, 8], P(('wide', 'grp')), may hold values from 0 to 2047
- seed_labels: int32 [32], replicated, may hold values from 0 to 524287
- coarse_first: int32 [524288], P(('wide', 'grp')), may hold values from 0 to 31
- coarse_second: int32 [524288, 1], P(('wide', 'grp')), may hold values from 0 to 31; in each aligned block of 2048 rows (0 to 2047, 2048 to 4095, ...) at most 80 rows name the same one
- sub_assign: int32 [524288], P(('wide', 'grp')), may hold values from 0 to 15
- group_map: int32 [32], replicated, may hold values from 0 to 63, as said below
Outputs:
- label_vectors: bfloat16 [524288, 768], P(('wide', 'grp'))
- coarse_centroids: float32 [32, 768], replicated
- sub_centroids: float32 [64, 16, 768], P('wide')
The draws below stay inside these ranges and needn't reach their ends.
Inputs may be any that keep to these rules, and one draw needn't show every extreme that they name: `inst_labels`: entries of block j of a device's rows name labels of the device with wide index j and the same grp index. `coarse_second`: among the 2048 labels of one device no cluster is named more than 80 times. `group_map`: no group hosts more than 1 clusters; one hosts exactly 1.
All inputs are finite; a program needn't handle non-finite values.
Results may differ from the reference program's by a relative error of at most 0.0054.
Values may be sent and summed in bfloat16 or wider, within the bound.
No kernel may reach another device: no remote copies, remote signals or barrier semaphores. Data moves between devices by JAX's collectives and lax.ppermute only.
A program may use at most 64 MiB of HBM per device.

```python
import math
import jax
import jax.numpy as jnp
import numpy as np
from jax import lax

D = 768
COARSE = 32
SUB = 16
TOPL = 8
LAB_DEV = 2048
ROWS_DEV = 1024
LABELS = 524288
INSTANCES = 262144
MOSTC = 80
HOSTC = 1
N_WIDE = 64
N_GRP = 4


def draw_group_map(key, part):
    key = jax.random.fold_in(key, 11)
    key_slots, key_shuffle = jax.random.split(key)
    slot_perm = jax.random.permutation(key_slots, N_WIDE * HOSTC)
    first_host = slot_perm[0] // HOSTC
    elsewhere = jnp.where(slot_perm // HOSTC != first_host, 0, 1)
    ordering = jnp.argsort(elsewhere, stable=True)
    picked_hosts = (slot_perm[ordering] // HOSTC)[:COARSE - HOSTC]
    host_list = jnp.concatenate([jnp.full((HOSTC,), first_host, dtype=jnp.int32), picked_hosts.astype(jnp.int32)])
    return jax.random.permutation(key_shuffle, host_list).astype(jnp.int32)


def with_ends(values, rng, smallest, top_value):
    extent = values.shape
    spot = [jax.random.randint(jax.random.fold_in(rng, axis), (), 0, extent[axis]) for axis in range(len(extent))]
    values = values.at[tuple(spot)].set(smallest)
    longest = extent.index(max(extent))
    spot[longest] = (spot[longest] + 1) % extent[longest]
    return values.at[tuple(spot)].set(top_value)


def steps_of(own_key, extent, cuts, least, largest):
    def one(position, parts):
        steps = jax.random.uniform(jax.random.fold_in(jax.random.fold_in(own_key, 6), position), (parts,), jnp.float32, least / len(cuts), largest / len(cuts))
        return jnp.repeat(jnp.exp(steps), extent[position] // parts).reshape((-1,) + (1,) * (len(extent) - position - 1))

    factor_of = one(*cuts[0])
    for cut in cuts[1:]:
        factor_of = factor_of * one(*cut)
    return factor_of


def routed_block(key, own, number, rows, number_of, top, most, lean):
    sequence = jax.random.permutation(key, number_of)
    heavy_load, usual = portions_of(number_of, rows * top, most, lean, True), portions_of(number_of, rows * top, most, lean, False)
    places = jnp.arange(number_of)

    def named(sizes, rotation):
        used = int((sizes > 0).sum())
        fixed = max(1, used // 4)
        passed = fixed + (places - fixed + rotation * (used - fixed)) % max(1, number_of - fixed)
        return jnp.zeros((number_of,), jnp.int32).at[sequence[jnp.where(places < fixed, places, passed)]].set(jnp.asarray(sizes, jnp.int32))

    sizes = jnp.where(number % 4 == 0, named(heavy_load, number // 4), named(usual, number - number // 4 - 1))
    mixed = jax.random.permutation(jax.random.fold_in(own, 3), number_of)
    giver, receiver = mixed[0:number_of // 2 * 2:2], mixed[1:number_of // 2 * 2:2]
    margin = jnp.minimum(sizes[giver] - 1, most - sizes[receiver]) // 2
    margin = jnp.where((giver == sequence[0]) | (receiver == sequence[0]) | (sizes[receiver] == 0), 0, jnp.maximum(margin, 0))
    passed = jax.random.randint(jax.random.fold_in(own, 4), (number_of // 2,), 0, 1 << 20) % (margin + 1)
    sizes = sizes.at[giver].add(-passed).at[receiver].add(passed)
    members = jnp.searchsorted(jnp.cumsum(sizes), jnp.arange(rows * top), side="right").astype(jnp.int32)
    table = members.reshape(top, rows).T
    table = table[jax.random.permutation(jax.random.fold_in(own, 1), rows)]
    rotation = jax.random.randint(jax.random.fold_in(own, 2), (rows, 1), 0, top)
    return jnp.take_along_axis(table, (jnp.arange(top)[None, :] + rotation) % top, axis=1)


def portions_of(count, total, bound, slope, full):
    loads = [(1 << 20) // math.isqrt(grade ** slope) + 1 for grade in range(1, count + 1)]
    largest = bound if full else min(bound, max(-(-total // count), total * loads[0] // sum(loads)))
    least = 1 if total - largest >= count - 1 else 0
    counts, rest = [largest] + [least] * (count - 1), total - largest - least * (count - 1)
    while rest > 0:
        candidates = [i for i in range(1, count) if counts[i] < largest] or [i for i in range(1, count) if counts[i] < bound]
        whole, left = sum([loads[i] for i in candidates]), rest
        for i in candidates:
            addition = min(bound - counts[i], max(1, left * loads[i] // whole), rest)
            counts[i] = counts[i] + addition
            rest = rest - addition
    return np.array(counts)


def noise(stream_key, dims, width, reach, pieces=(), kind=jnp.bfloat16):
    values = jax.random.normal(stream_key, dims, jnp.float32) * width
    if len(pieces) > 0:
        values = steps_of(stream_key, dims, pieces, -0.22, 0.18) * values
    return jnp.clip(values, min=-reach, max=reach).astype(kind)


def setup_inputs(seed: int = 0) -> dict:
    key_list = jax.random.split(jax.random.key(seed), 8)
    inst_rows = noise(key_list[0], (INSTANCES, D), 1.0, 6.0, ((0, 256),))
    inst_labels = with_ends(jax.random.randint(key_list[1], (INSTANCES, TOPL), 0, LAB_DEV), jax.random.fold_in(key_list[1], 1), 0, LAB_DEV - 1).astype(jnp.int32)
    seed_labels = with_ends(jax.random.randint(key_list[2], (COARSE,), 0, LABELS), jax.random.fold_in(key_list[2], 1), 0, LABELS - 1).astype(jnp.int32)
    coarse_first = with_ends(jax.random.randint(key_list[3], (LABELS,), 0, COARSE), jax.random.fold_in(key_list[3], 1), 0, COARSE - 1).astype(jnp.int32)
    coarse_second_keys = jax.random.split(jax.random.fold_in(key_list[4], 1), LABELS // LAB_DEV)
    coarse_second_turns = jax.random.permutation(jax.random.fold_in(key_list[4], 3), LABELS // LAB_DEV)
    coarse_second = jax.vmap(lambda own, number: routed_block(jax.random.fold_in(key_list[4], 2), own, number, LAB_DEV, COARSE, 1, MOSTC, 1))(coarse_second_keys, coarse_second_turns).reshape((LABELS, 1))
    sub_assign = with_ends(jax.random.randint(key_list[5], (LABELS,), 0, SUB), jax.random.fold_in(key_list[5], 1), 0, SUB - 1).astype(jnp.int32)
    group_map = draw_group_map(jax.random.fold_in(key_list[7], 71), 0)
    return {"inst_rows": inst_rows, "inst_labels": inst_labels, "seed_labels": seed_labels, "coarse_first": coarse_first, "coarse_second": coarse_second, "sub_assign": sub_assign, "group_map": group_map}


EPSILON = 1e-06
CONCENTRATION = 16.0

def rms_rows(matrix):
    return matrix * lax.rsqrt(lax.optimization_barrier(jnp.mean(matrix * matrix, axis=-1, keepdims=True)) + EPSILON)

def weighted_pass(blocks, centroids, assigned, cluster_total):
    cent_bf = centroids.astype(jnp.bfloat16)

    def block_step(running, inputs):
        block_rows, labels_here = inputs
        picked = cent_bf[labels_here].astype(jnp.float32)
        cosine = lax.optimization_barrier(jnp.sum(block_rows.astype(jnp.float32) * picked, axis=1)) / D
        weight = jnp.exp(CONCENTRATION * cosine).astype(jnp.bfloat16)
        weight = lax.optimization_barrier(weight).astype(jnp.float32)
        weighted_rows = weight[:, None] * block_rows.astype(jnp.float32)
        return (running + jax.ops.segment_sum(weighted_rows, labels_here, num_segments=cluster_total), None)
    running, _ = lax.scan(block_step, jnp.zeros((cluster_total, D), jnp.float32), (blocks, assigned))
    return rms_rows(running)

def plain_pass(blocks, assigned, cluster_total):

    def block_step(running, inputs):
        block_rows, labels_here = inputs
        return (running + jax.ops.segment_sum(block_rows.astype(jnp.float32), labels_here, num_segments=cluster_total), None)
    running, _ = lax.scan(block_step, jnp.zeros((cluster_total, D), jnp.float32), (blocks, assigned))
    return rms_rows(running)

def reference(inst_rows, inst_labels, seed_labels, coarse_first, coarse_second, sub_assign, group_map):
    devices = N_WIDE * N_GRP
    per_dest = ROWS_DEV // N_WIDE
    dest_rows = inst_rows.reshape(N_WIDE, N_GRP, N_WIDE, per_dest, D).transpose(2, 1, 0, 3, 4).reshape(devices, ROWS_DEV, D)
    dest_labels = inst_labels.reshape(N_WIDE, N_GRP, N_WIDE, per_dest, TOPL).transpose(2, 1, 0, 3, 4).reshape(devices, ROWS_DEV * TOPL)

    def label_sum(inputs):
        rows_here, labels_here = inputs
        repeated = jnp.repeat(rows_here.astype(jnp.float32), TOPL, axis=0)
        label_sums = jax.ops.segment_sum(repeated, labels_here, num_segments=LAB_DEV)
        return rms_rows(label_sums).astype(jnp.bfloat16)
    blocks = lax.map(label_sum, (dest_rows, dest_labels))
    label_vectors = blocks.reshape(LABELS, D)
    start_cent = rms_rows(label_vectors[seed_labels].astype(jnp.float32))
    first_cent = weighted_pass(blocks, start_cent, coarse_first.reshape(devices, LAB_DEV), COARSE)
    second = coarse_second[:, 0]
    coarse_centroids = weighted_pass(blocks, first_cent, second.reshape(devices, LAB_DEV), COARSE)
    sub_ids = (second * SUB + sub_assign).reshape(devices, LAB_DEV)
    sub_start = plain_pass(blocks, sub_ids, COARSE * SUB)
    sub_final = weighted_pass(blocks, sub_start, sub_ids, COARSE * SUB)
    cluster_ids = jnp.arange(COARSE, dtype=jnp.int32)
    same_host = group_map[:, None] == group_map[None, :]
    earlier = cluster_ids[None, :] < cluster_ids[:, None]
    host_rank = lax.optimization_barrier(jnp.sum(same_host & earlier, axis=1)).astype(jnp.int32)
    chosen = (group_map[None, None, :] == jnp.arange(N_WIDE, dtype=jnp.int32)[:, None, None]) & (host_rank[None, None, :] == jnp.arange(HOSTC, dtype=jnp.int32)[None, :, None])
    hosted = jnp.dot(chosen.astype(jnp.float32).reshape(N_WIDE * HOSTC, COARSE), sub_final.reshape(COARSE, SUB * D), precision=lax.Precision.HIGHEST)
    return (label_vectors, coarse_centroids, hosted.reshape(N_WIDE, HOSTC * SUB, D))
```

```python
import jax
import jax.numpy as jnp
from jax import lax
from jax.experimental import pallas as pl
from jax.experimental.pallas import tpu as pltpu
from jax.sharding import PartitionSpec as P

SUB = 16
EPSILON = 1e-06
CONCENTRATION = 16.0
TILE = 256
VMEM_LIMIT = 56 * 1024 * 1024

F32 = jnp.float32
BF16 = jnp.bfloat16


def rms_rows(matrix):
    return matrix * lax.rsqrt(jnp.mean(matrix * matrix, axis=-1, keepdims=True) + EPSILON)


def params():
    return pltpu.CompilerParams(
        dimension_semantics=("arbitrary",), vmem_limit_bytes=VMEM_LIMIT
    )


def whole(shape):
    return pl.BlockSpec(shape, lambda i: (0,) * len(shape))


def counts_kernel(labels_ref, out_ref):
    tile = pl.program_id(0)
    shape = out_ref.shape
    label = tile * shape[0] + lax.broadcasted_iota(jnp.int32, shape, 0)
    total = jnp.zeros(shape, F32)
    for slot in range(labels_ref.shape[0]):
        total = total + jnp.where(labels_ref[slot : slot + 1, :] == label, 1.0, 0.0)
    out_ref[...] = total.astype(BF16)


def label_counts(labels_by_slot, lab_dev):
    slots, rows = labels_by_slot.shape
    return pl.pallas_call(
        counts_kernel,
        grid=(lab_dev // TILE,),
        in_specs=[whole((slots, rows))],
        out_specs=pl.BlockSpec((TILE, rows), lambda i: (i, 0)),
        out_shape=jax.ShapeDtypeStruct((lab_dev, rows), BF16),
        compiler_params=params(),
        cost_estimate=pl.CostEstimate(
            flops=3 * slots * rows * lab_dev, bytes_accessed=2 * rows * lab_dev, transcendentals=0
        ),
        name="label_counts",
    )(labels_by_slot)


def weighted_part(centroids, vectors, ids_row, width):
    scores = lax.dot_general(
        centroids, vectors, (((1,), (1,)), ((), ())), preferred_element_type=F32
    )
    member = ids_row == lax.broadcasted_iota(jnp.int32, scores.shape, 0)
    cosine = jnp.sum(jnp.where(member, scores, 0.0), axis=0, keepdims=True) / width
    weight = jnp.exp(CONCENTRATION * cosine)
    weights = jnp.where(member, weight, 0.0).astype(BF16)
    return jnp.dot(weights, vectors, preferred_element_type=F32)


def label_kernel(counts_ref, rows_ref, start_ref, first_ref, sub_ref, lv_ref, m_ref, s_ref, s_acc):
    tile = pl.program_id(0)

    @pl.when(tile == 0)
    def _():
        m_ref[...] = jnp.zeros_like(m_ref)
        s_acc[...] = jnp.zeros_like(s_acc)

    sums = jnp.dot(counts_ref[...], rows_ref[...], preferred_element_type=F32)
    vectors = rms_rows(sums).astype(BF16)
    lv_ref[...] = vectors
    sub_member = sub_ref[0] == lax.broadcasted_iota(jnp.int32, (s_acc.shape[0], TILE), 0)
    s_acc[...] += jnp.dot(
        jnp.where(sub_member, 1.0, 0.0).astype(BF16), vectors, preferred_element_type=F32
    )
    m_ref[...] += weighted_part(start_ref[...], vectors, first_ref[0], vectors.shape[1])

    @pl.when(tile == pl.num_programs(0) - 1)
    def _():
        s_ref[...] = s_acc[...].astype(BF16)


def label_pass(counts, rows, start, first, sub, sub_total):
    lab_dev, row_total = counts.shape
    width = rows.shape[1]
    coarse = start.shape[0]
    return pl.pallas_call(
        label_kernel,
        grid=(lab_dev // TILE,),
        in_specs=[
            pl.BlockSpec((TILE, row_total), lambda i: (i, 0)),
            whole((row_total, width)),
            whole((coarse, width)),
            pl.BlockSpec((1, 1, TILE), lambda i: (i, 0, 0)),
            pl.BlockSpec((1, 1, TILE), lambda i: (i, 0, 0)),
        ],
        out_specs=[
            pl.BlockSpec((TILE, width), lambda i: (i, 0)),
            whole((coarse, width)),
            whole((sub_total, width)),
        ],
        out_shape=[
            jax.ShapeDtypeStruct((lab_dev, width), BF16),
            jax.ShapeDtypeStruct((coarse, width), F32),
            jax.ShapeDtypeStruct((sub_total, width), BF16),
        ],
        scratch_shapes=[pltpu.VMEM((sub_total, width), F32)],
        compiler_params=params(),
        name="label_pass",
    )(counts, rows, start, first, sub)


def pass_kernel(cent_ref, lv_ref, ids_ref, out_ref, acc):
    tile = pl.program_id(0)

    @pl.when(tile == 0)
    def _():
        acc[...] = jnp.zeros_like(acc)

    vectors = lv_ref[...]
    acc[...] += weighted_part(cent_ref[...], vectors, ids_ref[0], vectors.shape[1])

    @pl.when(tile == pl.num_programs(0) - 1)
    def _():
        out_ref[...] = acc[...].astype(out_ref.dtype)


def weighted_sums(centroids, vectors, ids, kind, name):
    lab_dev, width = vectors.shape
    total = centroids.shape[0]
    return pl.pallas_call(
        pass_kernel,
        grid=(lab_dev // TILE,),
        in_specs=[
            whole((total, width)),
            pl.BlockSpec((TILE, width), lambda i: (i, 0)),
            pl.BlockSpec((1, 1, TILE), lambda i: (i, 0, 0)),
        ],
        out_specs=whole((total, width)),
        out_shape=jax.ShapeDtypeStruct((total, width), kind),
        scratch_shapes=[pltpu.VMEM((total, width), F32)],
        compiler_params=params(),
        cost_estimate=pl.CostEstimate(
            flops=4 * total * lab_dev * width, bytes_accessed=2 * lab_dev * width, transcendentals=0
        ),
        name=name,
    )(centroids, vectors, ids)


def to_all(blocks):
    return lax.all_to_all(blocks, "wide", split_axis=0, concat_axis=0, tiled=True)


def spread(piece, n_wide):
    return jnp.broadcast_to(piece[None], (n_wide,) + piece.shape)


def grp_shift(value, step):
    n = lax.axis_size("grp")
    return lax.ppermute(value, "grp", [(i, (i + step) % n) for i in range(n)])


def grp_sum(value):
    others = [grp_shift(value, step) for step in range(1, lax.axis_size("grp"))]
    total = value.astype(F32)
    for other in others:
        total = total + other.astype(F32)
    return total


def grp_gather(value):
    n = lax.axis_size("grp")
    pieces = [value] + [grp_shift(value, n - step) for step in range(1, n)]
    return jnp.roll(jnp.stack(pieces), lax.axis_index("grp"), axis=0)


def grp_scatter(blocks):
    n = lax.axis_size("grp")
    me = lax.axis_index("grp")
    total = lax.dynamic_index_in_dim(blocks, me, 0, keepdims=False).astype(F32)
    for step in range(1, n):
        block = lax.dynamic_index_in_dim(blocks, lax.rem(me + step, n), 0, keepdims=False)
        total = total + grp_shift(block, step).astype(F32)
    return total


def halves(value):
    high = lax.reduce_precision(value, 8, 7)
    return high.astype(BF16), (value - high).astype(BF16)


def shards(inst_rows, inst_labels, seed_labels, coarse_first, coarse_second, sub_assign, group_map):
    n_wide = lax.axis_size("wide")
    n_grp = lax.axis_size("grp")
    lab_dev = coarse_first.shape[0]
    row_total, width = inst_rows.shape
    slots = inst_labels.shape[1]
    coarse = group_map.shape[0]
    per_dest = row_total // n_wide
    quarter = SUB // n_grp
    piece = coarse * width // n_wide
    me_grp = lax.axis_index("grp")
    lanes = 128

    block_base = (jnp.arange(row_total, dtype=jnp.int32) // per_dest * n_grp + me_grp) * lab_dev
    wanted = seed_labels[None, :] - block_base[:, None]
    seed_counts = jnp.zeros((row_total, coarse), F32)
    for slot in range(slots):
        seed_counts = seed_counts + (inst_labels[:, slot][:, None] == wanted)
    seed_part = lax.dot_general(
        seed_counts.astype(BF16), inst_rows, (((0,), (0,)), ((), ())), preferred_element_type=F32
    )
    by_slot = inst_labels.reshape(n_wide, per_dest, slots).transpose(0, 2, 1)
    sent = jnp.concatenate(
        [
            seed_part.reshape(n_wide, piece),
            by_slot.reshape(n_wide, slots * per_dest).astype(F32),
        ],
        axis=1,
    )
    early = to_all(sent)
    rows_in, early = lax.optimization_barrier((inst_rows, early))
    received = to_all(rows_in.reshape(n_wide, per_dest, width)).reshape(row_total, width)
    labels_by_slot = (
        early[:, piece:]
        .astype(jnp.int32)
        .reshape(n_wide, slots, per_dest)
        .transpose(1, 0, 2)
        .reshape(slots, row_total)
    )
    counts = label_counts(labels_by_slot, lab_dev)
    seed_piece = grp_sum(jnp.sum(early[:, :piece], axis=0))

    n_x, n_z, n_c = 4, 8, 2
    me_wide = lax.axis_index("wide")
    place = (me_wide // (n_z * n_c), me_wide // n_c % n_z, me_wide % n_c)
    gathered = seed_piece[None]
    for size, unit, here in ((n_c, 1, place[2]), (n_x, n_z * n_c, place[0]), (n_z, n_c, place[1])):
        pieces = [gathered]
        for step in range(1, size):
            pairs = []
            for source in range(n_wide):
                digit = source // unit % size
                pairs.append((source, source + ((digit - step) % size - digit) * unit))
            pieces.append(lax.ppermute(gathered, "wide", pairs))
        gathered = jnp.roll(jnp.stack(pieces), here, axis=0)
    seed_sums = gathered.reshape(n_z, n_x, n_c, piece).transpose(1, 0, 2, 3).reshape(coarse, width)
    start = rms_rows(lax.reduce_precision(rms_rows(seed_sums), 8, 7)).astype(BF16)

    second = coarse_second.reshape(lab_dev)
    sub_total = coarse * SUB
    sub_ids = (sub_assign // quarter) * (coarse * quarter) + second * quarter + sub_assign % quarter
    tiles = lab_dev // TILE
    first_ids = coarse_first.reshape(tiles, 1, TILE)
    second_ids = second.reshape(tiles, 1, TILE)
    sub_ids = sub_ids.reshape(tiles, 1, TILE)
    label_vectors, m_one, sub_part = label_pass(
        counts, received, start, first_ids, sub_ids, sub_total
    )

    m_one = grp_sum(m_one.astype(BF16))
    sub_mine = grp_scatter(sub_part.reshape(n_grp, coarse * quarter, width))
    chunk_m, chunk_s = piece // lanes, 2 * width // lanes
    pad = (-(chunk_m + chunk_s)) % 16
    sent = jnp.concatenate(
        [
            sub_mine.astype(BF16).reshape(n_wide, chunk_s, lanes),
            m_one.astype(BF16).reshape(n_wide, chunk_m, lanes),
            jnp.zeros((n_wide, pad, lanes), BF16),
        ],
        axis=1,
    )
    got = jnp.sum(to_all(sent).astype(F32), axis=0)

    sub_rows = rms_rows(got[:chunk_s].reshape(2, width)).astype(BF16)
    sent = jnp.concatenate(
        [
            sub_rows.reshape(chunk_s, lanes),
            got[chunk_s : chunk_s + chunk_m].astype(BF16),
            jnp.zeros((pad, lanes), BF16),
        ],
        axis=0,
    )
    got = to_all(spread(sent, n_wide))
    first = rms_rows(
        got[:, chunk_s : chunk_s + chunk_m].reshape(coarse, width).astype(F32)
    ).astype(BF16)
    sub_quarter = got[:, :chunk_s].reshape(coarse * quarter, width)

    m_two = weighted_sums(first, label_vectors, second_ids, F32, "second_pass")
    m_two = grp_sum(m_two)
    two_piece = jnp.sum(to_all(m_two.reshape(n_wide, piece)), axis=0)

    sub_start = grp_gather(sub_quarter).reshape(sub_total, width)
    w_sub = weighted_sums(sub_start, label_vectors, sub_ids, BF16, "sub_pass")
    w_mine = grp_scatter(w_sub.reshape(n_grp, coarse * quarter, width)).astype(BF16)
    host = (
        group_map[None, :] == lax.broadcasted_iota(jnp.int32, (n_wide, coarse), 0)
    ).astype(BF16)
    to_hosts = jnp.dot(
        host, w_mine.reshape(coarse, quarter * width), preferred_element_type=F32
    ).astype(BF16)
    chunk_w = quarter * width // lanes
    high, low = halves(two_piece.reshape(chunk_m, lanes))
    pad = (-(2 * chunk_m + chunk_w)) % 16
    sent = jnp.concatenate(
        [
            to_hosts.reshape(n_wide, chunk_w, lanes),
            spread(jnp.concatenate([high, low, jnp.zeros((pad, lanes), BF16)]), n_wide),
        ],
        axis=1,
    )
    got = to_all(sent)
    last = got[:, chunk_w : chunk_w + 2 * chunk_m].astype(F32)
    coarse_centroids = rms_rows(
        (last[:, :chunk_m] + last[:, chunk_m:]).reshape(coarse, width)
    )
    hosted = rms_rows(
        jnp.sum(got[:, :chunk_w].astype(F32), axis=0).reshape(quarter, width)
    )
    sub_centroids = grp_gather(hosted).reshape(1, SUB, width)
    return label_vectors, coarse_centroids, sub_centroids


def solution(mesh):
    in_specs = (
        P(("wide", "grp"), None),
        P(("wide", "grp"), None),
        P(),
        P(("wide", "grp")),
        P(("wide", "grp"), None),
        P(("wide", "grp")),
        P(),
    )
    out_specs = (P(("wide", "grp"), None), P(), P("wide", None, None))
    return jax.shard_map(shards, mesh=mesh, in_specs=in_specs, out_specs=out_specs, check_vma=False)
```

```python
import functools

import jax
import jax.numpy as jnp
from jax import lax
from jax.experimental import pallas as pl
from jax.experimental.pallas import tpu as pltpu
from jax.sharding import PartitionSpec as P

SUB = 16
EPSILON = 1e-06
CONCENTRATION = 16.0
TILE = 256
VMEM_LIMIT = 56 * 1024 * 1024

F32 = jnp.float32
BF16 = jnp.bfloat16


def rms_rows(matrix):
    return matrix * lax.rsqrt(jnp.mean(matrix * matrix, axis=-1, keepdims=True) + EPSILON)


def params():
    return pltpu.CompilerParams(
        dimension_semantics=("arbitrary",), vmem_limit_bytes=VMEM_LIMIT
    )


def whole(shape):
    return pl.BlockSpec(shape, lambda i: (0,) * len(shape))


def counts_kernel(labels_ref, out_ref):
    tile = pl.program_id(0)
    shape = out_ref.shape
    label = tile * shape[0] + lax.broadcasted_iota(jnp.int32, shape, 0)
    total = jnp.zeros(shape, F32)
    for slot in range(labels_ref.shape[0]):
        total = total + jnp.where(labels_ref[slot : slot + 1, :] == label, 1.0, 0.0)
    out_ref[...] = total.astype(BF16)


def label_counts(labels_by_slot, lab_dev):
    slots, rows = labels_by_slot.shape
    return pl.pallas_call(
        counts_kernel,
        grid=(lab_dev // TILE,),
        in_specs=[whole((slots, rows))],
        out_specs=pl.BlockSpec((TILE, rows), lambda i: (i, 0)),
        out_shape=jax.ShapeDtypeStruct((lab_dev, rows), BF16),
        compiler_params=params(),
        cost_estimate=pl.CostEstimate(
            flops=3 * slots * rows * lab_dev, bytes_accessed=2 * rows * lab_dev, transcendentals=0
        ),
        name="label_counts",
    )(labels_by_slot)


def weight_rows(centroids, vectors, ids_row):
    scores = lax.dot_general(
        centroids, vectors, (((1,), (1,)), ((), ())), preferred_element_type=F32
    )
    member = ids_row == lax.broadcasted_iota(jnp.int32, scores.shape, 0)
    cosine = jnp.sum(jnp.where(member, scores, 0.0), axis=0, keepdims=True) / vectors.shape[1]
    weight = jnp.exp(CONCENTRATION * cosine)
    return jnp.where(member, weight, 0.0).astype(BF16)


def label_kernel(counts_ref, rows_ref, sub_ref, lv_ref, *rest):
    blocks, (acc, before) = rest[:-2], rest[-2:]
    step = pl.program_id(0)
    sub_total, width = acc.shape
    quarter = sub_total // len(blocks)

    @pl.when(step == 0)
    def _():
        acc[...] = jnp.zeros_like(acc)
        before[...] = jnp.zeros_like(before)

    vectors = before[...]
    member = sub_ref[0] == lax.broadcasted_iota(jnp.int32, (sub_total, vectors.shape[0]), 0)
    sums = jnp.dot(counts_ref[...], rows_ref[:, :width], preferred_element_type=F32)
    acc[...] += jnp.dot(
        jnp.where(member, 1.0, 0.0).astype(BF16), vectors, preferred_element_type=F32
    )
    fresh = rms_rows(sums).astype(BF16)
    lv_ref[...] = fresh
    before[...] = fresh

    @pl.when(step == pl.num_programs(0) - 1)
    def _():
        for index, block in enumerate(blocks):
            block[...] = acc[index * quarter : (index + 1) * quarter].astype(BF16)


def label_pass(counts, rows, sub, width, sub_total, blocks):
    lab_dev, row_total = counts.shape
    tile = 512
    tiles = lab_dev // tile
    each = sub_total // blocks

    def now(i):
        return (jnp.minimum(i, tiles - 1), 0)

    return pl.pallas_call(
        label_kernel,
        grid=(tiles + 1,),
        in_specs=[
            pl.BlockSpec((tile, row_total), now),
            whole(rows.shape),
            pl.BlockSpec((1, 1, tile), lambda i: (jnp.maximum(i - 1, 0), 0, 0)),
        ],
        out_specs=[pl.BlockSpec((tile, width), now)] + [whole((each, width))] * blocks,
        out_shape=[jax.ShapeDtypeStruct((lab_dev, width), BF16)]
        + [jax.ShapeDtypeStruct((each, width), BF16)] * blocks,
        scratch_shapes=[
            pltpu.VMEM((sub_total, width), F32),
            pltpu.VMEM((tile, width), BF16),
        ],
        compiler_params=params(),
        cost_estimate=pl.CostEstimate(
            flops=2 * lab_dev * width * (row_total + sub_total),
            bytes_accessed=2 * lab_dev * (row_total + width),
            transcendentals=0,
        ),
        name="label_pass",
    )(counts, rows, sub.reshape(tiles, 1, tile))


def pass_kernel(cent_total, lv_ref, ids_ref, *rest):
    cents, outs, acc = rest[:cent_total], rest[cent_total:-1], rest[-1]
    step = pl.program_id(0)

    @pl.when(step == 0)
    def _():
        acc[...] = jnp.zeros_like(acc)

    vectors = lv_ref[...]
    centroids = jnp.concatenate([cent[...] for cent in cents], axis=0)
    acc[...] += jnp.dot(
        weight_rows(centroids, vectors, ids_ref[0]), vectors, preferred_element_type=F32
    )

    @pl.when(step == pl.num_programs(0) - 1)
    def _():
        each = acc.shape[0] // len(outs)
        for index, out in enumerate(outs):
            out[...] = acc[index * each : (index + 1) * each].astype(out.dtype)


def weighted_sums(centroids, vectors, ids, outs, kind, name):
    lab_dev, width = vectors.shape
    each = centroids[0].shape[0]
    total = each * len(centroids)
    share = total // outs
    tile = 1024
    tiles = lab_dev // tile
    return pl.pallas_call(
        functools.partial(pass_kernel, len(centroids)),
        grid=(tiles,),
        in_specs=[
            pl.BlockSpec((tile, width), lambda i: (i, 0)),
            pl.BlockSpec((1, 1, tile), lambda i: (i, 0, 0)),
        ]
        + [whole((each, width))] * len(centroids),
        out_specs=[whole((share, width))] * outs,
        out_shape=[jax.ShapeDtypeStruct((share, width), kind)] * outs,
        scratch_shapes=[pltpu.VMEM((total, width), F32)],
        compiler_params=params(),
        cost_estimate=pl.CostEstimate(
            flops=4 * total * lab_dev * width, bytes_accessed=2 * lab_dev * width, transcendentals=0
        ),
        name=name,
    )(vectors, ids.reshape(tiles, 1, tile), *centroids)


def to_all(blocks):
    return lax.all_to_all(blocks, "wide", split_axis=0, concat_axis=0, tiled=True)


def to_chips(blocks):
    n = lax.axis_size("wide")
    groups = [list(range(core, n, 2)) for core in range(2)]
    return lax.all_to_all(
        blocks, "wide", split_axis=0, concat_axis=0, axis_index_groups=groups, tiled=True
    )


def core_swap(value):
    n = lax.axis_size("wide")
    return lax.ppermute(value, "wide", [(i, i ^ 1) for i in range(n)])


def spread(piece, n_wide):
    return jnp.broadcast_to(piece[None], (n_wide,) + piece.shape)


def grp_shift(value, step):
    n = lax.axis_size("grp")
    return lax.ppermute(value, "grp", [(i, (i + step) % n) for i in range(n)])


def grp_sum(value):
    others = [grp_shift(value, step) for step in range(1, lax.axis_size("grp"))]
    total = value.astype(F32)
    for other in others:
        total = total + other.astype(F32)
    return total


def grp_gather(value):
    n = lax.axis_size("grp")
    return [value] + [grp_shift(value, n - step) for step in range(1, n)]


def grp_scatter(blocks):
    total = blocks[0].astype(F32)
    for step in range(1, len(blocks)):
        total = total + grp_shift(blocks[step], step).astype(F32)
    return total


def halves(value):
    high = lax.reduce_precision(value, 8, 7)
    return high.astype(BF16), (value - high).astype(BF16)


def shards(inst_rows, inst_labels, seed_labels, coarse_first, coarse_second, sub_assign, group_map):
    n_wide = lax.axis_size("wide")
    n_grp = lax.axis_size("grp")
    lab_dev = coarse_first.shape[0]
    row_total, width = inst_rows.shape
    slots = inst_labels.shape[1]
    coarse = group_map.shape[0]
    per_dest = row_total // n_wide
    piece = coarse * width // n_wide
    me_grp = lax.axis_index("grp")
    lanes = 128

    block_base = (jnp.arange(row_total, dtype=jnp.int32) // per_dest * n_grp + me_grp) * lab_dev
    wanted = seed_labels[None, :] - block_base[:, None]
    seed_counts = jnp.zeros((row_total, coarse), F32)
    for slot in range(slots):
        seed_counts = seed_counts + (inst_labels[:, slot][:, None] == wanted)
    seed_part = lax.dot_general(
        seed_counts.astype(BF16), inst_rows, (((0,), (0,)), ((), ())), preferred_element_type=F32
    )
    by_slot = inst_labels.reshape(n_wide, per_dest, slots).transpose(0, 2, 1)
    sent = jnp.concatenate(
        [
            seed_part.reshape(n_wide, piece),
            by_slot.reshape(n_wide, slots * per_dest).astype(F32),
        ],
        axis=1,
    )
    early = to_all(sent)
    labels_by_slot = (
        early[:, piece:]
        .astype(jnp.int32)
        .reshape(n_wide, slots, per_dest)
        .transpose(1, 0, 2)
        .reshape(slots, row_total)
    )
    counts = label_counts(labels_by_slot, lab_dev)

    chunk_m = piece // lanes
    high, low = halves(jnp.sum(early[:, :piece], axis=0).reshape(chunk_m, lanes))
    beside = jnp.concatenate(
        [high, low, jnp.zeros((per_dest - 2 * chunk_m, lanes), BF16)], axis=0
    )
    sent = jnp.concatenate(
        [inst_rows.reshape(n_wide, per_dest, width), spread(beside, n_wide)], axis=2
    )
    received = to_all(sent)
    seed_sums = received[:, : 2 * chunk_m, width:].astype(F32)
    seed_sums = (seed_sums[:, :chunk_m] + seed_sums[:, chunk_m:]).reshape(coarse, width)
    seed_rows = grp_sum(lax.reduce_precision(rms_rows(seed_sums), 8, 7).astype(BF16))
    start = rms_rows(seed_rows).astype(BF16)
    received = received.reshape(row_total, width + lanes)

    me_core = lax.rem(lax.axis_index("wide"), 2)
    second = coarse_second.reshape(lab_dev)
    sub_total = coarse * SUB
    share = SUB // 2 // n_grp
    each = coarse * share
    core_turn = (sub_assign // (SUB // 2)) ^ me_core
    grp_turn = lax.rem(sub_assign // share + (n_grp - me_grp), n_grp)
    sub_ids = (core_turn * n_grp + grp_turn) * each + second * share + sub_assign % share
    label_vectors, own_half, other_half = label_pass(
        counts, received, sub_ids, width, sub_total, 2
    )

    def reduced(own, other):
        half = own.astype(F32) + core_swap(other).astype(F32)
        half = half.astype(BF16)
        return grp_scatter([half[i * each : (i + 1) * each] for i in range(n_grp)]).astype(BF16)

    (m_one,) = weighted_sums([start], label_vectors, coarse_first, 1, BF16, "first_pass")
    sub_mine = reduced(own_half, other_half)
    m_one = grp_sum(m_one).astype(BF16)
    chips = n_wide // 2
    chunk_s, chunk_r = share * width // lanes, width // lanes
    pad = (-(chunk_s + chunk_r)) % 8
    sent = jnp.concatenate(
        [
            sub_mine.reshape(chips, chunk_s, lanes),
            m_one.reshape(chips, chunk_r, lanes),
            jnp.zeros((chips, pad, lanes), BF16),
        ],
        axis=1,
    )
    got = jnp.sum(to_chips(sent).astype(F32), axis=0)

    sub_rows = rms_rows(got[:chunk_s].reshape(share, width)).astype(BF16)
    sent = jnp.concatenate(
        [
            sub_rows.reshape(chunk_s, lanes),
            got[chunk_s : chunk_s + chunk_r].astype(BF16),
            jnp.zeros((pad, lanes), BF16),
        ],
        axis=0,
    )
    got = to_chips(spread(sent, chips))
    first = got[:, chunk_s : chunk_s + chunk_r].reshape(coarse, width)
    first = rms_rows(first.astype(F32) + core_swap(first).astype(F32)).astype(BF16)
    sub_own = got[:, :chunk_s].reshape(each, width)

    (m_two,) = weighted_sums([first], label_vectors, second, 1, F32, "second_pass")
    sub_own, m_two = lax.optimization_barrier((sub_own, m_two))
    m_two = grp_sum(m_two)
    two_piece = jnp.sum(to_all(m_two.reshape(n_wide, piece)), axis=0)

    sub_start = grp_gather(sub_own)
    sub_start = sub_start + [core_swap(block) for block in sub_start]
    w_own, w_other = weighted_sums(sub_start, label_vectors, sub_ids, 2, BF16, "sub_pass")
    w_mine = reduced(w_own, w_other)
    host = (
        group_map[None, :] == lax.broadcasted_iota(jnp.int32, (n_wide, coarse), 0)
    ).astype(BF16)
    to_hosts = jnp.dot(
        host, w_mine.reshape(coarse, share * width), preferred_element_type=F32
    ).astype(BF16)
    high, low = halves(two_piece.reshape(chunk_m, lanes))
    pad = (-(2 * chunk_m + chunk_s)) % 8
    sent = jnp.concatenate(
        [
            to_hosts.reshape(n_wide, chunk_s, lanes),
            spread(jnp.concatenate([high, low, jnp.zeros((pad, lanes), BF16)]), n_wide),
        ],
        axis=1,
    )
    got = to_all(sent)
    hosted = jnp.sum(got[:, :chunk_s].astype(F32).reshape(chips, 2, chunk_s, lanes), axis=0)
    hosted = rms_rows(hosted.reshape(2 * share, width))
    last = got[:, chunk_s : chunk_s + 2 * chunk_m].astype(F32)
    coarse_centroids = rms_rows(
        (last[:, :chunk_m] + last[:, chunk_m:]).reshape(coarse, width)
    )
    pieces = grp_gather(hosted)
    ordered = []
    for position in range(n_grp):
        turn = lax.rem(position + (n_grp - me_grp), n_grp)
        value = pieces[0]
        for index in range(1, n_grp):
            value = jnp.where(turn == index, pieces[index], value)
        ordered.append(value.reshape(2, 1, share, width))
    sub_centroids = jnp.concatenate(ordered, axis=1).reshape(1, SUB, width)
    return label_vectors, coarse_centroids, sub_centroids


def solution(mesh):
    in_specs = (
        P(("wide", "grp"), None),
        P(("wide", "grp"), None),
        P(),
        P(("wide", "grp")),
        P(("wide", "grp"), None),
        P(("wide", "grp")),
        P(),
    )
    out_specs = (P(("wide", "grp"), None), P(), P("wide", None, None))
    return jax.shard_map(shards, mesh=mesh, in_specs=in_specs, out_specs=out_specs, check_vma=False)
```

```python
import functools

import jax
import jax.numpy as jnp
from jax import lax
from jax.experimental import pallas as pl
from jax.experimental.pallas import tpu as pltpu
from jax.sharding import PartitionSpec as P

SUB = 16
EPSILON = 1e-06
CONCENTRATION = 16.0
TILE = 512
LANES = 128
PIECE = 96
VMEM_LIMIT = 56 * 1024 * 1024

F32 = jnp.float32
BF16 = jnp.bfloat16


def rms_rows(matrix):
    return matrix * lax.rsqrt(jnp.mean(matrix * matrix, axis=-1, keepdims=True) + EPSILON)


def params():
    return pltpu.CompilerParams(
        dimension_semantics=("arbitrary",), vmem_limit_bytes=VMEM_LIMIT
    )


def whole(shape):
    return pl.BlockSpec(shape, lambda i: (0,) * len(shape))


def sender_kernel(per_dest, span, labels_ref, rows_ref, seeds_ref, out_ref):
    slots, row_total = labels_ref.shape
    width = rows_ref.shape[1]
    coarse = seeds_ref.shape[0]
    labels = labels_ref[...]
    block = lax.broadcasted_iota(jnp.int32, (coarse, row_total), 1) // per_dest
    wanted = seeds_ref[...] - block * span
    counts = jnp.zeros((coarse, row_total), F32)
    for slot in range(slots):
        counts = counts + jnp.where(labels[slot : slot + 1, :] == wanted, 1.0, 0.0)
    part = jnp.dot(counts.astype(BF16), rows_ref[...], preferred_element_type=F32)
    high = part.astype(BF16)
    low = (part - high.astype(F32)).astype(BF16)
    filler = jnp.zeros((coarse, LANES - PIECE), BF16)
    pieces = width // PIECE
    table = []
    for value in (high, low):
        for index in range(pieces):
            chunk = value[:, index * PIECE : (index + 1) * PIECE]
            table.append(jnp.concatenate([chunk, filler], axis=1))
    table = jnp.concatenate(table, axis=0)
    row = lax.broadcasted_iota(jnp.int32, (row_total, 1), 0)
    dest, place = row // per_dest, row % per_dest
    each = pieces // 2
    index = (place // each * pieces + dest % 2 * each + place % each) * coarse + dest // 2
    index = jnp.where(place < 2 * each, index, -1)
    picked = lax.broadcasted_iota(jnp.int32, (row_total, table.shape[0]), 1) == index
    beside = jnp.dot(
        jnp.where(picked, 1.0, 0.0).astype(BF16), table, preferred_element_type=F32
    )
    digits = jnp.concatenate([labels // 256, labels % 256], axis=0).astype(F32)
    digits = digits.T.astype(BF16)
    shift = lax.broadcasted_iota(jnp.int32, (2 * slots, LANES), 0) + PIECE
    shift = shift == lax.broadcasted_iota(jnp.int32, (2 * slots, LANES), 1)
    beside = beside + jnp.dot(
        digits, jnp.where(shift, 1.0, 0.0).astype(BF16), preferred_element_type=F32
    )
    out_ref[:, :width] = rows_ref[...]
    out_ref[:, width:] = beside.astype(BF16)


def sender(labels, rows, seeds, per_dest, span):
    row_total, width = rows.shape
    return pl.pallas_call(
        functools.partial(sender_kernel, per_dest, span),
        grid=(1,),
        in_specs=[whole(labels.shape), whole(rows.shape), whole(seeds.shape)],
        out_specs=whole((row_total, width + LANES)),
        out_shape=jax.ShapeDtypeStruct((row_total, width + LANES), BF16),
        compiler_params=params(),
        name="sender",
    )(labels, rows, seeds)


def counts_kernel(beside_ref, out_ref, labels_ref):
    shape = out_ref.shape
    slots = labels_ref.shape[0]

    @pl.when(pl.program_id(0) == 0)
    def _():
        turned = beside_ref[...].astype(F32).T
        labels = turned[PIECE : PIECE + slots] * 256.0 + turned[PIECE + slots : PIECE + 2 * slots]
        labels_ref[...] = labels.astype(jnp.int32)

    labels = (labels_ref[...] - pl.program_id(0) * shape[0]).astype(jnp.int16)
    label = lax.broadcasted_iota(jnp.int32, shape, 0).astype(jnp.int16)
    one, zero = jnp.ones((), BF16), jnp.zeros((), BF16)
    total = jnp.zeros(shape, BF16)
    for slot in range(slots):
        named = jnp.broadcast_to(labels[slot : slot + 1, :], shape)
        total = total + jnp.where(named == label, one, zero)
    out_ref[...] = total


def label_counts(received, slots, lab_dev):
    rows, full = received.shape
    return pl.pallas_call(
        counts_kernel,
        grid=(lab_dev // TILE,),
        in_specs=[pl.BlockSpec((rows, LANES), lambda i: (0, full // LANES - 1))],
        out_specs=pl.BlockSpec((TILE, rows), lambda i: (i, 0)),
        out_shape=jax.ShapeDtypeStruct((lab_dev, rows), BF16),
        scratch_shapes=[pltpu.VMEM((slots, rows), jnp.int32)],
        compiler_params=params(),
        cost_estimate=pl.CostEstimate(
            flops=3 * slots * rows * lab_dev, bytes_accessed=2 * rows * lab_dev, transcendentals=0
        ),
        name="label_counts",
    )(received)


def weight_rows(centroids, vectors, ids_row):
    scores = lax.dot_general(
        centroids, vectors, (((1,), (1,)), ((), ())), preferred_element_type=F32
    )
    member = ids_row == lax.broadcasted_iota(jnp.int32, scores.shape, 0)
    cosine = jnp.sum(jnp.where(member, scores, 0.0), axis=0, keepdims=True) / vectors.shape[1]
    weight = jnp.exp(CONCENTRATION * cosine)
    return jnp.where(member, weight, 0.0).astype(BF16)


def label_kernel(counts_ref, rows_ref, sub_ref, lv_ref, *rest):
    blocks, (acc, before) = rest[:-2], rest[-2:]
    step = pl.program_id(0)
    sub_total, width = acc.shape
    quarter = sub_total // len(blocks)

    @pl.when(step == 0)
    def _():
        acc[...] = jnp.zeros_like(acc)
        before[...] = jnp.zeros_like(before)

    vectors = before[...]
    member = sub_ref[0] == lax.broadcasted_iota(jnp.int32, (sub_total, vectors.shape[0]), 0)
    sums = jnp.dot(counts_ref[...], rows_ref[:, :width], preferred_element_type=F32)
    acc[...] += jnp.dot(
        jnp.where(member, 1.0, 0.0).astype(BF16), vectors, preferred_element_type=F32
    )
    fresh = rms_rows(sums).astype(BF16)
    lv_ref[...] = fresh
    before[...] = fresh

    @pl.when(step == pl.num_programs(0) - 1)
    def _():
        for index, block in enumerate(blocks):
            block[...] = acc[index * quarter : (index + 1) * quarter].astype(BF16)


def label_pass(counts, rows, sub, width, sub_total, blocks):
    lab_dev, row_total = counts.shape
    tile = 512
    tiles = lab_dev // tile
    each = sub_total // blocks

    def now(i):
        return (jnp.minimum(i, tiles - 1), 0)

    return pl.pallas_call(
        label_kernel,
        grid=(tiles + 1,),
        in_specs=[
            pl.BlockSpec((tile, row_total), now),
            whole(rows.shape),
            pl.BlockSpec((1, 1, tile), lambda i: (jnp.maximum(i - 1, 0), 0, 0)),
        ],
        out_specs=[pl.BlockSpec((tile, width), now)] + [whole((each, width))] * blocks,
        out_shape=[jax.ShapeDtypeStruct((lab_dev, width), BF16)]
        + [jax.ShapeDtypeStruct((each, width), BF16)] * blocks,
        scratch_shapes=[
            pltpu.VMEM((sub_total, width), F32),
            pltpu.VMEM((tile, width), BF16),
        ],
        compiler_params=params(),
        cost_estimate=pl.CostEstimate(
            flops=2 * lab_dev * width * (row_total + sub_total),
            bytes_accessed=2 * lab_dev * (row_total + width),
            transcendentals=0,
        ),
        name="label_pass",
    )(counts, rows, sub.reshape(tiles, 1, tile))


def pass_kernel(cent_total, lv_ref, ids_ref, *rest):
    cents, outs, acc = rest[:cent_total], rest[cent_total:-1], rest[-1]
    step = pl.program_id(0)

    @pl.when(step == 0)
    def _():
        acc[...] = jnp.zeros_like(acc)

    vectors = lv_ref[...]
    centroids = jnp.concatenate([cent[...] for cent in cents], axis=0)
    acc[...] += jnp.dot(
        weight_rows(centroids, vectors, ids_ref[0]), vectors, preferred_element_type=F32
    )

    @pl.when(step == pl.num_programs(0) - 1)
    def _():
        each = acc.shape[0] // len(outs)
        for index, out in enumerate(outs):
            if len(out.shape) == 2:
                out[...] = acc[index * each : (index + 1) * each].astype(out.dtype)
            else:
                per_row = acc.shape[1] // out.shape[2]
                for place in range(out.shape[0]):
                    row, start = place // per_row, place % per_row * out.shape[2]
                    out[place] = acc[row : row + 1, start : start + out.shape[2]]


def weighted_sums(centroids, vectors, ids, outs, kind, name, shape=None):
    lab_dev, width = vectors.shape
    each = centroids[0].shape[0]
    total = each * len(centroids)
    share = total // outs
    tile = 1024
    tiles = lab_dev // tile
    return pl.pallas_call(
        functools.partial(pass_kernel, len(centroids)),
        grid=(tiles,),
        in_specs=[
            pl.BlockSpec((tile, width), lambda i: (i, 0)),
            pl.BlockSpec((1, 1, tile), lambda i: (i, 0, 0)),
        ]
        + [whole((each, width))] * len(centroids),
        out_specs=[whole(shape or (share, width))] * outs,
        out_shape=[jax.ShapeDtypeStruct(shape or (share, width), kind)] * outs,
        scratch_shapes=[pltpu.VMEM((total, width), F32)],
        compiler_params=params(),
        cost_estimate=pl.CostEstimate(
            flops=4 * total * lab_dev * width, bytes_accessed=2 * lab_dev * width, transcendentals=0
        ),
        name=name,
    )(vectors, ids.reshape(tiles, 1, tile), *centroids)


def to_all(blocks):
    return lax.all_to_all(blocks, "wide", split_axis=0, concat_axis=0, tiled=True)


def to_chips(blocks):
    n = lax.axis_size("wide")
    groups = [list(range(core, n, 2)) for core in range(2)]
    return lax.all_to_all(
        blocks, "wide", split_axis=0, concat_axis=0, axis_index_groups=groups, tiled=True
    )


def core_swap(value):
    n = lax.axis_size("wide")
    return lax.ppermute(value, "wide", [(i, i ^ 1) for i in range(n)])


def spread(piece, n_wide):
    return jnp.broadcast_to(piece[None], (n_wide,) + piece.shape)


def grp_shift(value, step):
    n = lax.axis_size("grp")
    return lax.ppermute(value, "grp", [(i, (i + step) % n) for i in range(n)])


def grp_sum(value):
    others = [grp_shift(value, step) for step in range(1, lax.axis_size("grp"))]
    total = value.astype(F32)
    for other in others:
        total = total + other.astype(F32)
    return total


def grp_gather(value):
    n = lax.axis_size("grp")
    return [value] + [grp_shift(value, n - step) for step in range(1, n)]


def grp_scatter(blocks):
    total = blocks[0].astype(F32)
    for step in range(1, len(blocks)):
        total = total + grp_shift(blocks[step], step).astype(F32)
    return total


def halves(value):
    high = lax.reduce_precision(value, 8, 7)
    return high.astype(BF16), (value - high).astype(BF16)


def shards(inst_rows, inst_labels, seed_labels, coarse_first, coarse_second, sub_assign, group_map):
    n_wide = lax.axis_size("wide")
    n_grp = lax.axis_size("grp")
    lab_dev = coarse_first.shape[0]
    row_total, width = inst_rows.shape
    slots = inst_labels.shape[1]
    coarse = group_map.shape[0]
    per_dest = row_total // n_wide
    piece = coarse * width // n_wide
    me_grp = lax.axis_index("grp")
    lanes = LANES
    chunk_m = piece // lanes

    sent = sender(
        inst_labels.T, inst_rows, (seed_labels - me_grp * lab_dev)[:, None], per_dest,
        n_grp * lab_dev,
    )
    received = to_all(sent.reshape(n_wide, per_dest, width + lanes))
    beside = received[:, :, width:].astype(F32)
    received = received.reshape(row_total, width + lanes)
    seed_piece = jnp.sum(beside, axis=0)[:, :PIECE]
    each = piece // PIECE
    seed_piece = (seed_piece[:each] + seed_piece[each : 2 * each]).reshape(1, piece)
    seed_piece = grp_sum(seed_piece)
    counts = label_counts(received, slots, lab_dev)
    seed_sums = to_all(spread(seed_piece, n_wide)).reshape(coarse, width)
    start = rms_rows(lax.reduce_precision(rms_rows(seed_sums), 8, 7)).astype(BF16)

    me_core = lax.rem(lax.axis_index("wide"), 2)
    second = coarse_second.reshape(lab_dev)
    sub_total = coarse * SUB
    share = SUB // 2 // n_grp
    each = coarse * share
    core_turn = (sub_assign // (SUB // 2)) ^ me_core
    grp_turn = lax.rem(sub_assign // share + (n_grp - me_grp), n_grp)
    sub_ids = (core_turn * n_grp + grp_turn) * each + second * share + sub_assign % share
    label_vectors, own_half, other_half = label_pass(
        counts, received, sub_ids, width, sub_total, 2
    )

    def reduced(own, other, *more):
        half = (own.astype(F32) + core_swap(other).astype(F32)).astype(BF16)
        return grp_scatter(
            [jnp.concatenate([half[i * each : (i + 1) * each], *more]) for i in range(n_grp)]
        )

    (m_one,) = weighted_sums([start], label_vectors, coarse_first, 1, BF16, "first_pass")
    sub_mine = reduced(own_half, other_half).astype(BF16)
    m_one = grp_sum(m_one).astype(BF16)
    chips = n_wide // 2
    sent = jnp.concatenate(
        [sub_mine.reshape(chips, share, width), m_one.reshape(chips, share, piece)], axis=2
    )
    got = jnp.sum(to_chips(sent).astype(F32), axis=0)

    sent = jnp.concatenate([rms_rows(got[:, :width]), got[:, width:]], axis=1).astype(BF16)
    got = to_chips(spread(sent, chips))
    first = got[:, :, width:].reshape(coarse, width)
    first = rms_rows(first.astype(F32) + core_swap(first).astype(F32)).astype(BF16)
    sub_own = got[:, :, :width].reshape(each, width)

    (m_two,) = weighted_sums(
        [first], label_vectors, second, 1, F32, "second_pass", (n_wide, 1, piece)
    )
    two_parts = to_all(m_two).reshape(n_wide, piece)

    sub_start = grp_gather(sub_own)
    _, *sub_start = lax.optimization_barrier((m_two, *sub_start))
    sub_start = sub_start + [core_swap(block) for block in sub_start]
    w_own, w_other = weighted_sums(sub_start, label_vectors, sub_ids, 2, BF16, "sub_pass")
    high, low = halves(jnp.sum(two_parts, axis=0))
    two_row = jnp.concatenate([high, low])[None]
    w_mine = reduced(w_own, w_other, jnp.pad(two_row, ((0, 7), (0, 0))))
    two_piece = w_mine[each, :piece] + w_mine[each, piece:]
    w_mine = w_mine[:each].astype(BF16)
    host = (
        group_map[None, :] == lax.broadcasted_iota(jnp.int32, (n_wide, coarse), 0)
    ).astype(BF16)
    to_hosts = jnp.dot(
        host, w_mine.reshape(coarse, share * width), preferred_element_type=F32
    ).astype(BF16)
    two_piece = jnp.stack(halves(two_piece))
    sent = jnp.concatenate(
        [to_hosts.reshape(n_wide, share, width), spread(two_piece, n_wide)], axis=2
    )
    got = to_all(sent).astype(F32)
    hosted = jnp.sum(got[:, :, :width].reshape(chips, 2, share, width), axis=0)
    hosted = rms_rows(hosted.reshape(2 * share, width))
    last = got[:, 0, width:] + got[:, 1, width:]
    coarse_centroids = rms_rows(last.reshape(coarse, width))
    pieces = grp_gather(hosted)
    ordered = []
    for position in range(n_grp):
        turn = lax.rem(position + (n_grp - me_grp), n_grp)
        value = pieces[0]
        for index in range(1, n_grp):
            value = jnp.where(turn == index, pieces[index], value)
        ordered.append(value.reshape(2, 1, share, width))
    sub_centroids = jnp.concatenate(ordered, axis=1).reshape(1, SUB, width)
    return label_vectors, coarse_centroids, sub_centroids


def solution(mesh):
    in_specs = (
        P(("wide", "grp"), None),
        P(("wide", "grp"), None),
        P(),
        P(("wide", "grp")),
        P(("wide", "grp"), None),
        P(("wide", "grp")),
        P(),
    )
    out_specs = (P(("wide", "grp"), None), P(), P("wide", None, None))
    return jax.shard_map(shards, mesh=mesh, in_specs=in_specs, out_specs=out_specs, check_vma=False)
```

```python
import functools

import jax
import jax.numpy as jnp
from jax import lax
from jax.experimental import pallas as pl
from jax.experimental.pallas import tpu as pltpu
from jax.sharding import PartitionSpec as P

SUB = 16
EPSILON = 1e-06
CONCENTRATION = 16.0
TILE = 512
LANES = 128
PIECE = 96
VMEM_LIMIT = 56 * 1024 * 1024

F32 = jnp.float32
BF16 = jnp.bfloat16


def rms_rows(matrix):
    return matrix * lax.rsqrt(jnp.mean(matrix * matrix, axis=-1, keepdims=True) + EPSILON)


def params():
    return pltpu.CompilerParams(
        dimension_semantics=("arbitrary",), vmem_limit_bytes=VMEM_LIMIT
    )


def whole(shape):
    return pl.BlockSpec(shape, lambda i: (0,) * len(shape))


def halved(rows, per_dest):
    total, width = rows.shape
    half = per_dest // 2
    parts = rows.astype(F32).reshape(total // per_dest, 2, half, width)
    return [parts[:, i].reshape(total // 2, width) for i in range(2)]


def sender_kernel(per_dest, lab_dev, labels_ref, rows_ref, seeds_ref, out_ref):
    slots, row_total = labels_ref.shape
    width = rows_ref.shape[1]
    coarse = seeds_ref.shape[1]
    labels = labels_ref[...]
    diagonal = lax.broadcasted_iota(jnp.int32, (coarse, coarse), 0)
    diagonal = diagonal == lax.broadcasted_iota(jnp.int32, (coarse, coarse), 1)
    seeds = jnp.where(diagonal, seeds_ref[...].astype(F32), 0.0)
    seeds = jnp.sum(seeds, axis=1, keepdims=True).astype(jnp.int32)
    block = lax.broadcasted_iota(jnp.int32, (coarse, row_total), 1) // per_dest
    owner = block * lax.axis_size("grp") + lax.axis_index("grp")
    wanted = seeds - owner * lab_dev
    counts = jnp.zeros((coarse, row_total), F32)
    for slot in range(slots):
        counts = counts + jnp.where(labels[slot : slot + 1, :] == wanted, 1.0, 0.0)
    part = jnp.dot(counts.astype(BF16), rows_ref[...], preferred_element_type=F32)
    high = part.astype(BF16)
    low = (part - high.astype(F32)).astype(BF16)
    filler = jnp.zeros((coarse, LANES - PIECE), BF16)
    pieces = width // PIECE
    table = []
    for value in (high, low):
        for index in range(pieces):
            chunk = value[:, index * PIECE : (index + 1) * PIECE]
            table.append(jnp.concatenate([chunk, filler], axis=1))
    table = jnp.concatenate(table, axis=0)
    half = per_dest // 2
    row = lax.broadcasted_iota(jnp.int32, (row_total // 2, 1), 0)
    dest, place = row // half, row % half
    each = pieces // 2
    index = (place // each * pieces + dest % 2 * each + place % each) * coarse + dest // 2
    picked = lax.broadcasted_iota(jnp.int32, (row_total // 2, table.shape[0]), 1) == index
    beside = jnp.dot(
        jnp.where(picked, 1.0, 0.0).astype(BF16), table, preferred_element_type=F32
    )
    digits = jnp.concatenate([labels // 256, labels % 256], axis=0).astype(F32)
    shape = (2 * slots, LANES)
    for index, part in enumerate(halved(digits.T, per_dest)):
        shift = lax.broadcasted_iota(jnp.int32, shape, 0) + PIECE + index * 2 * slots
        shift = shift == lax.broadcasted_iota(jnp.int32, shape, 1)
        beside = beside + jnp.dot(
            part.astype(BF16),
            jnp.where(shift, 1.0, 0.0).astype(BF16),
            preferred_element_type=F32,
        )
    for index, part in enumerate(halved(rows_ref[...], per_dest)):
        out_ref[:, index * width : (index + 1) * width] = part.astype(BF16)
    out_ref[:, 2 * width :] = beside.astype(BF16)


def sender(labels, rows, seeds, per_dest, lab_dev):
    row_total, width = rows.shape
    shape = (row_total // 2, 2 * width + LANES)
    return pl.pallas_call(
        functools.partial(sender_kernel, per_dest, lab_dev),
        grid=(1,),
        in_specs=[whole(labels.shape), whole(rows.shape), whole(seeds.shape)],
        out_specs=whole(shape),
        out_shape=jax.ShapeDtypeStruct(shape, BF16),
        compiler_params=params(),
        name="sender",
    )(labels, rows, seeds)


def counts_kernel(beside_ref, out_ref, labels_ref):
    shape = out_ref.shape
    slots = labels_ref.shape[0]

    @pl.when(pl.program_id(0) == 0)
    def _():
        turned = beside_ref[...].astype(F32).T
        half = turned.shape[1]
        for index in range(2):
            first = PIECE + index * 2 * slots
            labels = turned[first : first + slots] * 256.0
            labels = labels + turned[first + slots : first + 2 * slots]
            labels_ref[:, index * half : (index + 1) * half] = labels.astype(jnp.int32)

    labels = (labels_ref[...] - pl.program_id(0) * shape[0]).astype(jnp.int16)
    label = lax.broadcasted_iota(jnp.int32, shape, 0).astype(jnp.int16)
    one, zero = jnp.ones((), BF16), jnp.zeros((), BF16)
    total = jnp.zeros(shape, BF16)
    for slot in range(slots):
        named = jnp.broadcast_to(labels[slot : slot + 1, :], shape)
        total = total + jnp.where(named == label, one, zero)
    out_ref[...] = total


def label_counts(received, slots, lab_dev):
    half, full = received.shape
    rows = 2 * half
    return pl.pallas_call(
        counts_kernel,
        grid=(lab_dev // TILE,),
        in_specs=[pl.BlockSpec((half, LANES), lambda i: (0, full // LANES - 1))],
        out_specs=pl.BlockSpec((TILE, rows), lambda i: (i, 0)),
        out_shape=jax.ShapeDtypeStruct((lab_dev, rows), BF16),
        scratch_shapes=[pltpu.VMEM((slots, rows), jnp.int32)],
        compiler_params=params(),
        cost_estimate=pl.CostEstimate(
            flops=3 * slots * rows * lab_dev, bytes_accessed=2 * rows * lab_dev, transcendentals=0
        ),
        name="label_counts",
    )(received)


def weight_rows(centroids, vectors, ids_row):
    scores = lax.dot_general(
        centroids, vectors, (((1,), (1,)), ((), ())), preferred_element_type=F32
    )
    member = ids_row == lax.broadcasted_iota(jnp.int32, scores.shape, 0)
    cosine = jnp.sum(jnp.where(member, scores, 0.0), axis=0, keepdims=True) / vectors.shape[1]
    weight = jnp.exp(CONCENTRATION * cosine)
    return jnp.where(member, weight, 0.0).astype(BF16)


def label_kernel(
    counts_ref, rows_ref, sub_ref, lv_ref, own_ref, other_ref, acc, before
):
    step, last = pl.program_id(0), pl.num_programs(0) - 1
    sub_total, width = acc.shape

    def label_part():
        half = rows_ref.shape[0]
        sums = jnp.dot(counts_ref[:, :half], rows_ref[:, :width], preferred_element_type=F32)
        sums = sums + jnp.dot(
            counts_ref[:, half:], rows_ref[:, width : 2 * width], preferred_element_type=F32
        )
        return rms_rows(sums).astype(BF16)

    def sums_part():
        vectors = before[...]
        member = sub_ref[0] == lax.broadcasted_iota(jnp.int32, (sub_total, vectors.shape[0]), 0)
        return jnp.dot(
            jnp.where(member, 1.0, 0.0).astype(BF16), vectors, preferred_element_type=F32
        )

    @pl.when(step == 0)
    def _():
        acc[...] = jnp.zeros_like(acc)
        fresh = label_part()
        lv_ref[...] = fresh
        before[...] = fresh

    @pl.when(jnp.logical_and(step > 0, step < last))
    def _():
        fresh = label_part()
        acc[...] += sums_part()
        lv_ref[...] = fresh
        before[...] = fresh

    @pl.when(step == last)
    def _():
        total = acc[...] + sums_part()
        half = sub_total // 2
        own_ref[...] = total[:half].astype(BF16)
        other_ref[...] = total[half:].astype(BF16)


def label_pass(counts, rows, sub, width, sub_total):
    lab_dev, row_total = counts.shape
    tile = 512
    tiles = lab_dev // tile
    half = sub_total // 2

    def now(i):
        return (jnp.minimum(i, tiles - 1), 0)

    return pl.pallas_call(
        label_kernel,
        grid=(tiles + 1,),
        in_specs=[
            pl.BlockSpec((tile, row_total), now),
            whole(rows.shape),
            pl.BlockSpec((1, 1, tile), lambda i: (jnp.maximum(i - 1, 0), 0, 0)),
        ],
        out_specs=[pl.BlockSpec((tile, width), now), whole((half, width)), whole((half, width))],
        out_shape=[
            jax.ShapeDtypeStruct((lab_dev, width), BF16),
            jax.ShapeDtypeStruct((half, width), BF16),
            jax.ShapeDtypeStruct((half, width), BF16),
        ],
        scratch_shapes=[pltpu.VMEM((sub_total, width), F32), pltpu.VMEM((tile, width), BF16)],
        compiler_params=params(),
        cost_estimate=pl.CostEstimate(
            flops=2 * lab_dev * width * (row_total + sub_total),
            bytes_accessed=2 * lab_dev * (row_total + width),
            transcendentals=0,
        ),
        name="label_pass",
    )(counts, rows, sub.reshape(tiles, 1, tile))


def first_kernel(seed_ref, lv_ref, ids_ref, out_ref, acc, start):
    step = pl.program_id(0)

    @pl.when(step == 0)
    def _():
        acc[...] = jnp.zeros_like(acc)
        vectors = seed_ref[...].astype(BF16).astype(F32)
        start[...] = rms_rows(vectors).astype(BF16)

    vectors = lv_ref[...]
    acc[...] += jnp.dot(
        weight_rows(start[...], vectors, ids_ref[0]), vectors, preferred_element_type=F32
    )

    @pl.when(step == pl.num_programs(0) - 1)
    def _():
        out_ref[...] = acc[...].astype(BF16)


def first_pass(seeds, vectors, ids, coarse):
    lab_dev, width = vectors.shape
    tile = 1024
    tiles = lab_dev // tile
    return pl.pallas_call(
        first_kernel,
        grid=(tiles,),
        in_specs=[
            whole(seeds.shape),
            pl.BlockSpec((tile, width), lambda i: (i, 0)),
            pl.BlockSpec((1, 1, tile), lambda i: (i, 0, 0)),
        ],
        out_specs=whole((coarse, width)),
        out_shape=jax.ShapeDtypeStruct((coarse, width), BF16),
        scratch_shapes=[pltpu.VMEM((coarse, width), F32), pltpu.VMEM((coarse, width), BF16)],
        compiler_params=params(),
        cost_estimate=pl.CostEstimate(
            flops=4 * coarse * lab_dev * width, bytes_accessed=2 * lab_dev * width, transcendentals=0
        ),
        name="first_pass",
    )(seeds, vectors, ids.reshape(tiles, 1, tile))


def second_kernel(mine_ref, theirs_ref, lv_ref, ids_ref, out_ref, acc, cent):
    step = pl.program_id(0)

    @pl.when(step == 0)
    def _():
        acc[...] = jnp.zeros_like(acc)
        total = mine_ref[...].astype(F32) + theirs_ref[...].astype(F32)
        cent[...] = rms_rows(total).astype(BF16)

    vectors = lv_ref[...]
    acc[...] += jnp.dot(
        weight_rows(cent[...], vectors, ids_ref[0]), vectors, preferred_element_type=F32
    )

    @pl.when(step == pl.num_programs(0) - 1)
    def _():
        piece = out_ref.shape[2]
        per_row = acc.shape[1] // piece
        for place in range(out_ref.shape[0]):
            row, col = place // per_row, place % per_row * piece
            out_ref[place] = acc[row : row + 1, col : col + piece]


def second_pass(mine, theirs, vectors, ids, shape):
    lab_dev, width = vectors.shape
    coarse = mine.shape[0]
    tile = 1024
    tiles = lab_dev // tile
    return pl.pallas_call(
        second_kernel,
        grid=(tiles,),
        in_specs=[
            whole((coarse, width)),
            whole((coarse, width)),
            pl.BlockSpec((tile, width), lambda i: (i, 0)),
            pl.BlockSpec((1, 1, tile), lambda i: (i, 0, 0)),
        ],
        out_specs=whole(shape),
        out_shape=jax.ShapeDtypeStruct(shape, F32),
        scratch_shapes=[pltpu.VMEM((coarse, width), F32), pltpu.VMEM((coarse, width), BF16)],
        compiler_params=params(),
        cost_estimate=pl.CostEstimate(
            flops=4 * coarse * lab_dev * width, bytes_accessed=2 * lab_dev * width, transcendentals=0
        ),
        name="second_pass",
    )(mine, theirs, vectors, ids.reshape(tiles, 1, tile))


def pass_kernel(cent_total, lv_ref, ids_ref, *rest):
    cents, outs, acc = rest[:cent_total], rest[cent_total:-1], rest[-1]
    step = pl.program_id(0)

    @pl.when(step == 0)
    def _():
        acc[...] = jnp.zeros_like(acc)

    vectors = lv_ref[...]
    centroids = jnp.concatenate([cent[...] for cent in cents], axis=0)
    acc[...] += jnp.dot(
        weight_rows(centroids, vectors, ids_ref[0]), vectors, preferred_element_type=F32
    )

    @pl.when(step == pl.num_programs(0) - 1)
    def _():
        each = acc.shape[0] // len(outs)
        for index, out in enumerate(outs):
            out[...] = acc[index * each : (index + 1) * each].astype(out.dtype)


def weighted_sums(centroids, vectors, ids, outs, kind, name):
    lab_dev, width = vectors.shape
    each = centroids[0].shape[0]
    total = each * len(centroids)
    share = total // outs
    tile = 1024
    tiles = lab_dev // tile
    return pl.pallas_call(
        functools.partial(pass_kernel, len(centroids)),
        grid=(tiles,),
        in_specs=[
            pl.BlockSpec((tile, width), lambda i: (i, 0)),
            pl.BlockSpec((1, 1, tile), lambda i: (i, 0, 0)),
        ]
        + [whole((each, width))] * len(centroids),
        out_specs=[whole((share, width))] * outs,
        out_shape=[jax.ShapeDtypeStruct((share, width), kind)] * outs,
        scratch_shapes=[pltpu.VMEM((total, width), F32)],
        compiler_params=params(),
        cost_estimate=pl.CostEstimate(
            flops=4 * total * lab_dev * width, bytes_accessed=2 * lab_dev * width, transcendentals=0
        ),
        name=name,
    )(vectors, ids.reshape(tiles, 1, tile), *centroids)


def to_all(blocks):
    return lax.all_to_all(blocks, "wide", split_axis=0, concat_axis=0, tiled=True)


def to_chips(blocks):
    n = lax.axis_size("wide")
    groups = [list(range(core, n, 2)) for core in range(2)]
    return lax.all_to_all(
        blocks, "wide", split_axis=0, concat_axis=0, axis_index_groups=groups, tiled=True
    )


def core_swap(value):
    n = lax.axis_size("wide")
    return lax.ppermute(value, "wide", [(i, i ^ 1) for i in range(n)])


def spread(piece, n_wide):
    return jnp.broadcast_to(piece[None], (n_wide,) + piece.shape)


def grp_shift(value, step):
    n = lax.axis_size("grp")
    return lax.ppermute(value, "grp", [(i, (i + step) % n) for i in range(n)])


def grp_sum(value):
    others = [grp_shift(value, step) for step in range(1, lax.axis_size("grp"))]
    total = value.astype(F32)
    for other in others:
        total = total + other.astype(F32)
    return total


def grp_gather(value):
    n = lax.axis_size("grp")
    return [value] + [grp_shift(value, n - step) for step in range(1, n)]


def grp_scatter(blocks):
    total = blocks[0].astype(F32)
    for step in range(1, len(blocks)):
        total = total + grp_shift(blocks[step], step).astype(F32)
    return total


def halves(value):
    high = lax.reduce_precision(value, 8, 7)
    return high.astype(BF16), (value - high).astype(BF16)


def shards(inst_rows, inst_labels, seed_labels, coarse_first, coarse_second, sub_assign, group_map):
    n_wide = lax.axis_size("wide")
    n_grp = lax.axis_size("grp")
    lab_dev = coarse_first.shape[0]
    row_total, width = inst_rows.shape
    slots = inst_labels.shape[1]
    coarse = group_map.shape[0]
    per_dest = row_total // n_wide
    piece = coarse * width // n_wide
    me_grp = lax.axis_index("grp")
    lanes = LANES
    chunk_m = piece // lanes

    sent = sender(inst_labels.T, inst_rows, seed_labels[None], per_dest, lab_dev)
    received = to_all(sent.reshape(n_wide, per_dest // 2, 2 * width + lanes))
    beside = received[:, :, 2 * width :].astype(F32)
    received = received.reshape(row_total // 2, 2 * width + lanes)
    seed_piece = jnp.sum(beside, axis=0)[:, :PIECE]
    each = piece // PIECE
    seed_piece = (seed_piece[:each] + seed_piece[each : 2 * each]).reshape(1, piece)
    seed_piece = grp_sum(seed_piece)
    counts = label_counts(received, slots, lab_dev)
    seed_sums = to_all(spread(seed_piece, n_wide))

    me_core = lax.rem(lax.axis_index("wide"), 2)
    second = coarse_second.reshape(lab_dev)
    sub_total = coarse * SUB
    share = SUB // 2 // n_grp
    each = coarse * share
    core_turn = (sub_assign // (SUB // 2)) ^ me_core
    grp_turn = lax.rem(sub_assign // share + (n_grp - me_grp), n_grp)
    sub_ids = (core_turn * n_grp + grp_turn) * each + second * share + sub_assign % share
    label_vectors, own_half, other_half = label_pass(counts, received, sub_ids, width, sub_total)

    def reduced(own, other, *more):
        half = (own.astype(F32) + core_swap(other).astype(F32)).astype(BF16)
        return grp_scatter(
            [jnp.concatenate([half[i * each : (i + 1) * each], *more]) for i in range(n_grp)]
        )

    m_one = first_pass(rms_rows(seed_sums.reshape(coarse, width)), label_vectors, coarse_first, coarse)
    parts = reduced(own_half, other_half, m_one).astype(BF16)
    sub_mine, m_one = parts[:each], parts[each:]
    chips = n_wide // 2
    sent = jnp.concatenate(
        [sub_mine.reshape(chips, share, width), m_one.reshape(chips, share, piece)], axis=2
    )
    got = jnp.sum(to_chips(sent).astype(F32), axis=0)

    sent = jnp.concatenate([rms_rows(got[:, :width]), got[:, width:]], axis=1).astype(BF16)
    got = to_chips(spread(sent, chips))
    first = got[:, :, width:].reshape(coarse, width)
    sub_own = got[:, :, :width].reshape(each, width)

    m_two = second_pass(
        first, core_swap(first), label_vectors, second, (n_wide, 1, piece)
    )
    two_parts = to_all(m_two).reshape(n_wide, piece)

    sub_start = grp_gather(sub_own)
    _, *sub_start = lax.optimization_barrier((m_two, *sub_start))
    sub_start = sub_start + [core_swap(block) for block in sub_start]
    w_own, w_other = weighted_sums(sub_start, label_vectors, sub_ids, 2, BF16, "sub_pass")
    high, low = halves(jnp.sum(two_parts, axis=0))
    two_row = jnp.concatenate([high, low])[None]
    w_mine = reduced(w_own, w_other, jnp.pad(two_row, ((0, 7), (0, 0))))
    two_piece = w_mine[each, :piece] + w_mine[each, piece:]
    w_mine = w_mine[:each].astype(BF16)
    host = (
        group_map[None, :] == lax.broadcasted_iota(jnp.int32, (n_wide, coarse), 0)
    ).astype(BF16)
    to_hosts = jnp.dot(
        host, w_mine.reshape(coarse, share * width), preferred_element_type=F32
    ).astype(BF16)
    two_piece = jnp.stack(halves(two_piece))
    sent = jnp.concatenate(
        [to_hosts.reshape(n_wide, share, width), spread(two_piece, n_wide)], axis=2
    )
    got = to_all(sent).astype(F32)
    hosted = jnp.sum(got[:, :, :width].reshape(chips, 2, share, width), axis=0)
    hosted = rms_rows(hosted.reshape(2 * share, width))
    last = got[:, 0, width:] + got[:, 1, width:]
    coarse_centroids = rms_rows(last.reshape(coarse, width))
    pieces = grp_gather(hosted)
    ordered = []
    for position in range(n_grp):
        turn = lax.rem(position + (n_grp - me_grp), n_grp)
        value = pieces[0]
        for index in range(1, n_grp):
            value = jnp.where(turn == index, pieces[index], value)
        ordered.append(value.reshape(2, 1, share, width))
    sub_centroids = jnp.concatenate(ordered, axis=1).reshape(1, SUB, width)
    return label_vectors, coarse_centroids, sub_centroids


def solution(mesh):
    in_specs = (
        P(("wide", "grp"), None),
        P(("wide", "grp"), None),
        P(),
        P(("wide", "grp")),
        P(("wide", "grp"), None),
        P(("wide", "grp")),
        P(),
    )
    out_specs = (P(("wide", "grp"), None), P(), P("wide", None, None))
    return jax.shard_map(shards, mesh=mesh, in_specs=in_specs, out_specs=out_specs, check_vma=False)
```

```python
import functools

import jax
import jax.numpy as jnp
from jax import lax
from jax.experimental import pallas as pl
from jax.experimental.pallas import tpu as pltpu
from jax.sharding import PartitionSpec as P

SUB = 16
EPSILON = 1e-06
CONCENTRATION = 16.0
TILE = 512
LANES = 128
PIECE = 96
VMEM_LIMIT = 56 * 1024 * 1024

F32 = jnp.float32
BF16 = jnp.bfloat16


def rms_rows(matrix):
    return matrix * lax.rsqrt(jnp.mean(matrix * matrix, axis=-1, keepdims=True) + EPSILON)


def params():
    return pltpu.CompilerParams(
        dimension_semantics=("arbitrary",), vmem_limit_bytes=VMEM_LIMIT
    )


def whole(shape):
    return pl.BlockSpec(shape, lambda i: (0,) * len(shape))


def halved(rows, per_dest):
    total, width = rows.shape
    half = per_dest // 2
    parts = rows.astype(F32).reshape(total // per_dest, 2, half, width)
    return [parts[:, i].reshape(total // 2, width) for i in range(2)]


def sender_kernel(per_dest, lab_dev, labels_ref, rows_ref, seeds_ref, out_ref):
    slots, row_total = labels_ref.shape
    width = rows_ref.shape[1]
    coarse = seeds_ref.shape[1]
    labels = labels_ref[...]
    diagonal = lax.broadcasted_iota(jnp.int32, (coarse, coarse), 0)
    diagonal = diagonal == lax.broadcasted_iota(jnp.int32, (coarse, coarse), 1)
    seeds = jnp.where(diagonal, seeds_ref[...].astype(F32), 0.0)
    seeds = jnp.sum(seeds, axis=1, keepdims=True).astype(jnp.int32)
    block = lax.broadcasted_iota(jnp.int32, (coarse, row_total), 1) // per_dest
    owner = block * lax.axis_size("grp") + lax.axis_index("grp")
    wanted = seeds - owner * lab_dev
    counts = jnp.zeros((coarse, row_total), F32)
    for slot in range(slots):
        counts = counts + jnp.where(labels[slot : slot + 1, :] == wanted, 1.0, 0.0)
    part = jnp.dot(counts.astype(BF16), rows_ref[...], preferred_element_type=F32)
    high = part.astype(BF16)
    low = (part - high.astype(F32)).astype(BF16)
    filler = jnp.zeros((coarse, LANES - PIECE), BF16)
    pieces = width // PIECE
    table = []
    for value in (high, low):
        for index in range(pieces):
            chunk = value[:, index * PIECE : (index + 1) * PIECE]
            table.append(jnp.concatenate([chunk, filler], axis=1))
    table = jnp.concatenate(table, axis=0)
    half = per_dest // 2
    row = lax.broadcasted_iota(jnp.int32, (row_total // 2, 1), 0)
    dest, place = row // half, row % half
    each = pieces // 2
    index = (place // each * pieces + dest % 2 * each + place % each) * coarse + dest // 2
    picked = lax.broadcasted_iota(jnp.int32, (row_total // 2, table.shape[0]), 1) == index
    beside = jnp.dot(
        jnp.where(picked, 1.0, 0.0).astype(BF16), table, preferred_element_type=F32
    )
    digits = jnp.concatenate([labels // 256, labels % 256], axis=0).astype(F32)
    shape = (2 * slots, LANES)
    for index, part in enumerate(halved(digits.T, per_dest)):
        shift = lax.broadcasted_iota(jnp.int32, shape, 0) + PIECE + index * 2 * slots
        shift = shift == lax.broadcasted_iota(jnp.int32, shape, 1)
        beside = beside + jnp.dot(
            part.astype(BF16),
            jnp.where(shift, 1.0, 0.0).astype(BF16),
            preferred_element_type=F32,
        )
    for index, part in enumerate(halved(rows_ref[...], per_dest)):
        out_ref[:, index * width : (index + 1) * width] = part.astype(BF16)
    out_ref[:, 2 * width :] = beside.astype(BF16)


def sender(labels, rows, seeds, per_dest, lab_dev):
    row_total, width = rows.shape
    shape = (row_total // 2, 2 * width + LANES)
    return pl.pallas_call(
        functools.partial(sender_kernel, per_dest, lab_dev),
        grid=(1,),
        in_specs=[whole(labels.shape), whole(rows.shape), whole(seeds.shape)],
        out_specs=whole(shape),
        out_shape=jax.ShapeDtypeStruct(shape, BF16),
        compiler_params=params(),
        name="sender",
    )(labels, rows, seeds)


def counts_kernel(beside_ref, out_ref, labels_ref):
    shape = out_ref.shape
    slots = labels_ref.shape[0]

    @pl.when(pl.program_id(0) == 0)
    def _():
        turned = beside_ref[...].astype(F32).T
        half = turned.shape[1]
        for index in range(2):
            first = PIECE + index * 2 * slots
            labels = turned[first : first + slots] * 256.0
            labels = labels + turned[first + slots : first + 2 * slots]
            labels_ref[:, index * half : (index + 1) * half] = labels.astype(jnp.int32)

    labels = (labels_ref[...] - pl.program_id(0) * shape[0]).astype(jnp.int16)
    label = lax.broadcasted_iota(jnp.int32, shape, 0).astype(jnp.int16)
    one, zero = jnp.ones((), BF16), jnp.zeros((), BF16)
    total = jnp.zeros(shape, BF16)
    for slot in range(slots):
        named = jnp.broadcast_to(labels[slot : slot + 1, :], shape)
        total = total + jnp.where(named == label, one, zero)
    out_ref[...] = total


def label_counts(received, slots, lab_dev):
    half, full = received.shape
    rows = 2 * half
    return pl.pallas_call(
        counts_kernel,
        grid=(lab_dev // TILE,),
        in_specs=[pl.BlockSpec((half, LANES), lambda i: (0, full // LANES - 1))],
        out_specs=pl.BlockSpec((TILE, rows), lambda i: (i, 0)),
        out_shape=jax.ShapeDtypeStruct((lab_dev, rows), BF16),
        scratch_shapes=[pltpu.VMEM((slots, rows), jnp.int32)],
        compiler_params=params(),
        cost_estimate=pl.CostEstimate(
            flops=3 * slots * rows * lab_dev, bytes_accessed=2 * rows * lab_dev, transcendentals=0
        ),
        name="label_counts",
    )(received)


def weight_rows(centroids, vectors, ids_row):
    scores = lax.dot_general(
        centroids, vectors, (((1,), (1,)), ((), ())), preferred_element_type=F32
    )
    member = ids_row == lax.broadcasted_iota(jnp.int32, scores.shape, 0)
    cosine = jnp.sum(jnp.where(member, scores, 0.0), axis=0, keepdims=True) / vectors.shape[1]
    weight = jnp.exp(CONCENTRATION * cosine)
    return jnp.where(member, weight, 0.0).astype(BF16)


def label_kernel(
    counts_ref, rows_ref, sub_ref, lv_ref, own_ref, other_ref, acc, before
):
    step, last = pl.program_id(0), pl.num_programs(0) - 1
    sub_total, width = acc.shape

    def label_part():
        half = rows_ref.shape[0]
        sums = jnp.dot(counts_ref[:, :half], rows_ref[:, :width], preferred_element_type=F32)
        sums = sums + jnp.dot(
            counts_ref[:, half:], rows_ref[:, width : 2 * width], preferred_element_type=F32
        )
        return rms_rows(sums).astype(BF16)

    def sums_part():
        vectors = before[...]
        member = sub_ref[0] == lax.broadcasted_iota(jnp.int32, (sub_total, vectors.shape[0]), 0)
        return jnp.dot(
            jnp.where(member, 1.0, 0.0).astype(BF16), vectors, preferred_element_type=F32
        )

    @pl.when(step == 0)
    def _():
        acc[...] = jnp.zeros_like(acc)
        fresh = label_part()
        lv_ref[...] = fresh
        before[...] = fresh

    @pl.when(jnp.logical_and(step > 0, step < last))
    def _():
        fresh = label_part()
        acc[...] += sums_part()
        lv_ref[...] = fresh
        before[...] = fresh

    @pl.when(step == last)
    def _():
        total = acc[...] + sums_part()
        half = sub_total // 2
        own_ref[...] = total[:half].astype(BF16)
        other_ref[...] = total[half:].astype(BF16)


def label_pass(counts, rows, sub, width, sub_total):
    lab_dev, row_total = counts.shape
    tile = 512
    tiles = lab_dev // tile
    half = sub_total // 2

    def now(i):
        return (jnp.minimum(i, tiles - 1), 0)

    return pl.pallas_call(
        label_kernel,
        grid=(tiles + 1,),
        in_specs=[
            pl.BlockSpec((tile, row_total), now),
            whole(rows.shape),
            pl.BlockSpec((1, 1, tile), lambda i: (jnp.maximum(i - 1, 0), 0, 0)),
        ],
        out_specs=[pl.BlockSpec((tile, width), now), whole((half, width)), whole((half, width))],
        out_shape=[
            jax.ShapeDtypeStruct((lab_dev, width), BF16),
            jax.ShapeDtypeStruct((half, width), BF16),
            jax.ShapeDtypeStruct((half, width), BF16),
        ],
        scratch_shapes=[pltpu.VMEM((sub_total, width), F32), pltpu.VMEM((tile, width), BF16)],
        compiler_params=params(),
        cost_estimate=pl.CostEstimate(
            flops=2 * lab_dev * width * (row_total + sub_total),
            bytes_accessed=2 * lab_dev * (row_total + width),
            transcendentals=0,
        ),
        name="label_pass",
    )(counts, rows, sub.reshape(tiles, 1, tile))


def first_kernel(seed_ref, lv_ref, ids_ref, out_ref, acc, start):
    step = pl.program_id(0)

    @pl.when(step == 0)
    def _():
        acc[...] = jnp.zeros_like(acc)
        vectors = seed_ref[...].astype(BF16).astype(F32)
        start[...] = rms_rows(vectors).astype(BF16)

    vectors = lv_ref[...]
    acc[...] += jnp.dot(
        weight_rows(start[...], vectors, ids_ref[0]), vectors, preferred_element_type=F32
    )

    @pl.when(step == pl.num_programs(0) - 1)
    def _():
        out_ref[...] = acc[...].astype(BF16)


def first_pass(seeds, vectors, ids, coarse):
    lab_dev, width = vectors.shape
    tile = 1024
    tiles = lab_dev // tile
    return pl.pallas_call(
        first_kernel,
        grid=(tiles,),
        in_specs=[
            whole(seeds.shape),
            pl.BlockSpec((tile, width), lambda i: (i, 0)),
            pl.BlockSpec((1, 1, tile), lambda i: (i, 0, 0)),
        ],
        out_specs=whole((coarse, width)),
        out_shape=jax.ShapeDtypeStruct((coarse, width), BF16),
        scratch_shapes=[pltpu.VMEM((coarse, width), F32), pltpu.VMEM((coarse, width), BF16)],
        compiler_params=params(),
        cost_estimate=pl.CostEstimate(
            flops=4 * coarse * lab_dev * width, bytes_accessed=2 * lab_dev * width, transcendentals=0
        ),
        name="first_pass",
    )(seeds, vectors, ids.reshape(tiles, 1, tile))


def second_kernel(mine_ref, theirs_ref, lv_ref, ids_ref, out_ref, acc, cent):
    step = pl.program_id(0)

    @pl.when(step == 0)
    def _():
        acc[...] = jnp.zeros_like(acc)
        total = mine_ref[...].astype(F32) + theirs_ref[...].astype(F32)
        cent[...] = rms_rows(total).astype(BF16)

    vectors = lv_ref[...]
    acc[...] += jnp.dot(
        weight_rows(cent[...], vectors, ids_ref[0]), vectors, preferred_element_type=F32
    )

    @pl.when(step == pl.num_programs(0) - 1)
    def _():
        piece = out_ref.shape[2]
        per_row = acc.shape[1] // piece
        for place in range(out_ref.shape[0]):
            row, col = place // per_row, place % per_row * piece
            out_ref[place] = acc[row : row + 1, col : col + piece]


def second_pass(mine, theirs, vectors, ids, shape):
    lab_dev, width = vectors.shape
    coarse = mine.shape[0]
    tile = 1024
    tiles = lab_dev // tile
    return pl.pallas_call(
        second_kernel,
        grid=(tiles,),
        in_specs=[
            whole((coarse, width)),
            whole((coarse, width)),
            pl.BlockSpec((tile, width), lambda i: (i, 0)),
            pl.BlockSpec((1, 1, tile), lambda i: (i, 0, 0)),
        ],
        out_specs=whole(shape),
        out_shape=jax.ShapeDtypeStruct(shape, F32),
        scratch_shapes=[pltpu.VMEM((coarse, width), F32), pltpu.VMEM((coarse, width), BF16)],
        compiler_params=params(),
        cost_estimate=pl.CostEstimate(
            flops=4 * coarse * lab_dev * width, bytes_accessed=2 * lab_dev * width, transcendentals=0
        ),
        name="second_pass",
    )(mine, theirs, vectors, ids.reshape(tiles, 1, tile))


def pass_kernel(cent_total, lv_ref, ids_ref, *rest):
    cents, outs, acc = rest[:cent_total], rest[cent_total:-1], rest[-1]
    step = pl.program_id(0)

    @pl.when(step == 0)
    def _():
        acc[...] = jnp.zeros_like(acc)

    vectors = lv_ref[...]
    centroids = jnp.concatenate([cent[...] for cent in cents], axis=0)
    acc[...] += jnp.dot(
        weight_rows(centroids, vectors, ids_ref[0]), vectors, preferred_element_type=F32
    )

    @pl.when(step == pl.num_programs(0) - 1)
    def _():
        each = acc.shape[0] // len(outs)
        for index, out in enumerate(outs):
            out[...] = acc[index * each : (index + 1) * each].astype(out.dtype)


def weighted_sums(centroids, vectors, ids, outs, kind, name):
    lab_dev, width = vectors.shape
    each = centroids[0].shape[0]
    total = each * len(centroids)
    share = total // outs
    tile = 1024
    tiles = lab_dev // tile
    return pl.pallas_call(
        functools.partial(pass_kernel, len(centroids)),
        grid=(tiles,),
        in_specs=[
            pl.BlockSpec((tile, width), lambda i: (i, 0)),
            pl.BlockSpec((1, 1, tile), lambda i: (i, 0, 0)),
        ]
        + [whole((each, width))] * len(centroids),
        out_specs=[whole((share, width))] * outs,
        out_shape=[jax.ShapeDtypeStruct((share, width), kind)] * outs,
        scratch_shapes=[pltpu.VMEM((total, width), F32)],
        compiler_params=params(),
        cost_estimate=pl.CostEstimate(
            flops=4 * total * lab_dev * width, bytes_accessed=2 * lab_dev * width, transcendentals=0
        ),
        name=name,
    )(vectors, ids.reshape(tiles, 1, tile), *centroids)


def to_all(blocks):
    return lax.all_to_all(blocks, "wide", split_axis=0, concat_axis=0, tiled=True)


def to_chips(blocks):
    n = lax.axis_size("wide")
    groups = [list(range(core, n, 2)) for core in range(2)]
    return lax.all_to_all(
        blocks, "wide", split_axis=0, concat_axis=0, axis_index_groups=groups, tiled=True
    )


def core_swap(value):
    n = lax.axis_size("wide")
    return lax.ppermute(value, "wide", [(i, i ^ 1) for i in range(n)])


def spread(piece, n_wide):
    return jnp.broadcast_to(piece[None], (n_wide,) + piece.shape)


def grp_shift(value, step):
    n = lax.axis_size("grp")
    return lax.ppermute(value, "grp", [(i, (i + step) % n) for i in range(n)])


def total_of(own, others):
    own, first, second, third = (value.astype(F32) for value in (own, *others))
    return (own + second) + (first + third)


def grp_sum(value):
    return total_of(value, [grp_shift(value, step) for step in (1, 2, 3)])


def grp_gather(value):
    n = lax.axis_size("grp")
    return [value] + [grp_shift(value, n - step) for step in range(1, n)]


def grp_scatter(blocks):
    return total_of(blocks[0], [grp_shift(blocks[step], step) for step in (1, 2, 3)])


def halves(value):
    high = lax.reduce_precision(value, 8, 7)
    return high.astype(BF16), (value - high).astype(BF16)


def shards(inst_rows, inst_labels, seed_labels, coarse_first, coarse_second, sub_assign, group_map):
    n_wide = lax.axis_size("wide")
    n_grp = lax.axis_size("grp")
    lab_dev = coarse_first.shape[0]
    row_total, width = inst_rows.shape
    slots = inst_labels.shape[1]
    coarse = group_map.shape[0]
    per_dest = row_total // n_wide
    piece = coarse * width // n_wide
    me_grp = lax.axis_index("grp")
    lanes = LANES
    chunk_m = piece // lanes

    sent = sender(inst_labels.T, inst_rows, seed_labels[None], per_dest, lab_dev)
    received = to_all(sent.reshape(n_wide, per_dest // 2, 2 * width + lanes))
    beside = received[:, :, 2 * width :].astype(F32)
    received = received.reshape(row_total // 2, 2 * width + lanes)
    seed_piece = jnp.sum(beside, axis=0)[:, :PIECE]
    each = piece // PIECE
    seed_piece = (seed_piece[:each] + seed_piece[each : 2 * each]).reshape(1, piece)
    seed_piece = grp_sum(seed_piece)
    counts = label_counts(received, slots, lab_dev)
    seed_sums = to_all(spread(seed_piece, n_wide))

    me_core = lax.rem(lax.axis_index("wide"), 2)
    second = coarse_second.reshape(lab_dev)
    sub_total = coarse * SUB
    share = SUB // 2 // n_grp
    each = coarse * share
    core_turn = (sub_assign // (SUB // 2)) ^ me_core
    grp_turn = lax.rem(sub_assign // share + (n_grp - me_grp), n_grp)
    sub_ids = (core_turn * n_grp + grp_turn) * each + second * share + sub_assign % share
    label_vectors, own_half, other_half = label_pass(counts, received, sub_ids, width, sub_total)

    def reduced(own, other, *more):
        half = (own.astype(F32) + core_swap(other).astype(F32)).astype(BF16)
        return grp_scatter(
            [jnp.concatenate([half[i * each : (i + 1) * each], *more]) for i in range(n_grp)]
        )

    m_one = first_pass(rms_rows(seed_sums.reshape(coarse, width)), label_vectors, coarse_first, coarse)
    parts = reduced(own_half, other_half, m_one).astype(BF16)
    sub_mine, m_one = parts[:each], parts[each:]
    chips = n_wide // 2
    sent = jnp.concatenate(
        [sub_mine.reshape(chips, share, width), m_one.reshape(chips, share, piece)], axis=2
    )
    got = jnp.sum(to_chips(sent).astype(F32), axis=0)

    sent = jnp.concatenate([rms_rows(got[:, :width]), got[:, width:]], axis=1).astype(BF16)
    got = to_chips(spread(sent, chips))
    first = got[:, :, width:].reshape(coarse, width)
    sub_own = got[:, :, :width].reshape(each, width)

    theirs, sub_own = lax.optimization_barrier((core_swap(first), sub_own))
    m_two = second_pass(first, theirs, label_vectors, second, (n_wide, 1, piece))
    two_parts = to_all(m_two).reshape(n_wide, piece)

    sub_start = grp_gather(sub_own)
    _, *sub_start = lax.optimization_barrier((m_two, *sub_start))
    sub_start = sub_start + [core_swap(block) for block in sub_start]
    w_own, w_other = weighted_sums(sub_start, label_vectors, sub_ids, 2, BF16, "sub_pass")
    high, low = halves(jnp.sum(two_parts, axis=0))
    two_row = jnp.concatenate([high, low])[None]
    w_mine = reduced(w_own, w_other, jnp.pad(two_row, ((0, 7), (0, 0))))
    two_piece = w_mine[each, :piece] + w_mine[each, piece:]
    w_mine = w_mine[:each].astype(BF16)
    host = (
        group_map[None, :] == lax.broadcasted_iota(jnp.int32, (n_wide, coarse), 0)
    ).astype(BF16)
    to_hosts = jnp.dot(
        host, w_mine.reshape(coarse, share * width), preferred_element_type=F32
    ).astype(BF16)
    two_piece = jnp.stack(halves(two_piece))
    sent = jnp.concatenate(
        [to_hosts.reshape(n_wide, share, width), spread(two_piece, n_wide)], axis=2
    )
    got = to_all(sent).astype(F32)
    hosted = jnp.sum(got[:, :, :width].reshape(chips, 2, share, width), axis=0)
    hosted = rms_rows(hosted.reshape(2 * share, width))
    last = got[:, 0, width:] + got[:, 1, width:]
    coarse_centroids = rms_rows(last.reshape(coarse, width))
    pieces = grp_gather(hosted)
    ordered = []
    for position in range(n_grp):
        turn = lax.rem(position + (n_grp - me_grp), n_grp)
        value = pieces[0]
        for index in range(1, n_grp):
            value = jnp.where(turn == index, pieces[index], value)
        ordered.append(value.reshape(2, 1, share, width))
    sub_centroids = jnp.concatenate(ordered, axis=1).reshape(1, SUB, width)
    return label_vectors, coarse_centroids, sub_centroids


def solution(mesh):
    in_specs = (
        P(("wide", "grp"), None),
        P(("wide", "grp"), None),
        P(),
        P(("wide", "grp")),
        P(("wide", "grp"), None),
        P(("wide", "grp")),
        P(),
    )
    out_specs = (P(("wide", "grp"), None), P(), P("wide", None, None))
    return jax.shard_map(shards, mesh=mesh, in_specs=in_specs, out_specs=out_specs, check_vma=False)
```

```python
import functools

import jax
import jax.numpy as jnp
from jax import lax
from jax.experimental import pallas as pl
from jax.experimental.pallas import tpu as pltpu
from jax.sharding import PartitionSpec as P

SUB = 16
EPSILON = 1e-06
CONCENTRATION = 16.0
TILE = 512
LANES = 128
PIECE = 96
VMEM_LIMIT = 56 * 1024 * 1024

F32 = jnp.float32
BF16 = jnp.bfloat16


def rms_rows(matrix):
    return matrix * lax.rsqrt(jnp.mean(matrix * matrix, axis=-1, keepdims=True) + EPSILON)


def params():
    return pltpu.CompilerParams(
        dimension_semantics=("arbitrary",), vmem_limit_bytes=VMEM_LIMIT
    )


def whole(shape):
    return pl.BlockSpec(shape, lambda i: (0,) * len(shape))


def halved(rows, per_dest):
    total, width = rows.shape
    half = per_dest // 2
    parts = rows.astype(F32).reshape(total // per_dest, 2, half, width)
    return [parts[:, i].reshape(total // 2, width) for i in range(2)]


def sender_kernel(per_dest, lab_dev, labels_ref, rows_ref, seeds_ref, out_ref):
    slots, row_total = labels_ref.shape
    width = rows_ref.shape[1]
    coarse = seeds_ref.shape[1]
    labels = labels_ref[...]
    diagonal = lax.broadcasted_iota(jnp.int32, (coarse, coarse), 0)
    diagonal = diagonal == lax.broadcasted_iota(jnp.int32, (coarse, coarse), 1)
    seeds = jnp.where(diagonal, seeds_ref[...].astype(F32), 0.0)
    seeds = jnp.sum(seeds, axis=1, keepdims=True).astype(jnp.int32)
    block = lax.broadcasted_iota(jnp.int32, (coarse, row_total), 1) // per_dest
    owner = block * lax.axis_size("grp") + lax.axis_index("grp")
    wanted = seeds - owner * lab_dev
    counts = jnp.zeros((coarse, row_total), F32)
    for slot in range(slots):
        counts = counts + jnp.where(labels[slot : slot + 1, :] == wanted, 1.0, 0.0)
    part = jnp.dot(counts.astype(BF16), rows_ref[...], preferred_element_type=F32)
    high = part.astype(BF16)
    low = (part - high.astype(F32)).astype(BF16)
    filler = jnp.zeros((coarse, LANES - PIECE), BF16)
    pieces = width // PIECE
    table = []
    for value in (high, low):
        for index in range(pieces):
            chunk = value[:, index * PIECE : (index + 1) * PIECE]
            table.append(jnp.concatenate([chunk, filler], axis=1))
    table = jnp.concatenate(table, axis=0)
    half = per_dest // 2
    row = lax.broadcasted_iota(jnp.int32, (row_total // 2, 1), 0)
    dest, place = row // half, row % half
    each = pieces // 2
    index = (place // each * pieces + dest % 2 * each + place % each) * coarse + dest // 2
    picked = lax.broadcasted_iota(jnp.int32, (row_total // 2, table.shape[0]), 1) == index
    beside = jnp.dot(
        jnp.where(picked, 1.0, 0.0).astype(BF16), table, preferred_element_type=F32
    )
    digits = jnp.concatenate([labels // 256, labels % 256], axis=0).astype(F32)
    shape = (2 * slots, LANES)
    for index, part in enumerate(halved(digits.T, per_dest)):
        shift = lax.broadcasted_iota(jnp.int32, shape, 0) + PIECE + index * 2 * slots
        shift = shift == lax.broadcasted_iota(jnp.int32, shape, 1)
        beside = beside + jnp.dot(
            part.astype(BF16),
            jnp.where(shift, 1.0, 0.0).astype(BF16),
            preferred_element_type=F32,
        )
    for index, part in enumerate(halved(rows_ref[...], per_dest)):
        out_ref[:, index * width : (index + 1) * width] = part.astype(BF16)
    out_ref[:, 2 * width :] = beside.astype(BF16)


def sender(labels, rows, seeds, per_dest, lab_dev):
    row_total, width = rows.shape
    shape = (row_total // 2, 2 * width + LANES)
    return pl.pallas_call(
        functools.partial(sender_kernel, per_dest, lab_dev),
        grid=(1,),
        in_specs=[whole(labels.shape), whole(rows.shape), whole(seeds.shape)],
        out_specs=whole(shape),
        out_shape=jax.ShapeDtypeStruct(shape, BF16),
        compiler_params=params(),
        name="sender",
    )(labels, rows, seeds)


def counts_kernel(beside_ref, out_ref, labels_ref):
    shape = out_ref.shape
    slots = labels_ref.shape[0]

    @pl.when(pl.program_id(0) == 0)
    def _():
        turned = beside_ref[...].astype(F32).T
        half = turned.shape[1]
        for index in range(2):
            first = PIECE + index * 2 * slots
            labels = turned[first : first + slots] * 256.0
            labels = labels + turned[first + slots : first + 2 * slots]
            labels_ref[:, index * half : (index + 1) * half] = labels.astype(jnp.int32)

    labels = (labels_ref[...] - pl.program_id(0) * shape[0]).astype(jnp.int16)
    label = lax.broadcasted_iota(jnp.int32, shape, 0).astype(jnp.int16)
    one, zero = jnp.ones((), BF16), jnp.zeros((), BF16)
    total = jnp.zeros(shape, BF16)
    for slot in range(slots):
        named = jnp.broadcast_to(labels[slot : slot + 1, :], shape)
        total = total + jnp.where(named == label, one, zero)
    out_ref[...] = total


def label_counts(received, slots, lab_dev):
    half, full = received.shape
    rows = 2 * half
    return pl.pallas_call(
        counts_kernel,
        grid=(lab_dev // TILE,),
        in_specs=[pl.BlockSpec((half, LANES), lambda i: (0, full // LANES - 1))],
        out_specs=pl.BlockSpec((TILE, rows), lambda i: (i, 0)),
        out_shape=jax.ShapeDtypeStruct((lab_dev, rows), BF16),
        scratch_shapes=[pltpu.VMEM((slots, rows), jnp.int32)],
        compiler_params=params(),
        cost_estimate=pl.CostEstimate(
            flops=3 * slots * rows * lab_dev, bytes_accessed=2 * rows * lab_dev, transcendentals=0
        ),
        name="label_counts",
    )(received)


def weight_rows(centroids, vectors, ids_row):
    scores = lax.dot_general(
        centroids, vectors, (((1,), (1,)), ((), ())), preferred_element_type=F32
    )
    member = ids_row == lax.broadcasted_iota(jnp.int32, scores.shape, 0)
    cosine = jnp.sum(jnp.where(member, scores, 0.0), axis=0, keepdims=True) / vectors.shape[1]
    weight = jnp.exp(CONCENTRATION * cosine)
    return jnp.where(member, weight, 0.0).astype(BF16)


def label_kernel(
    counts_ref, rows_ref, sub_ref, lv_ref, own_ref, other_ref, acc, before
):
    step, last = pl.program_id(0), pl.num_programs(0) - 1
    sub_total, width = acc.shape

    def label_part():
        half = rows_ref.shape[0]
        sums = jnp.dot(counts_ref[:, :half], rows_ref[:, :width], preferred_element_type=F32)
        sums = sums + jnp.dot(
            counts_ref[:, half:], rows_ref[:, width : 2 * width], preferred_element_type=F32
        )
        return rms_rows(sums).astype(BF16)

    def sums_part():
        vectors = before[...]
        member = sub_ref[0] == lax.broadcasted_iota(jnp.int32, (sub_total, vectors.shape[0]), 0)
        return jnp.dot(
            jnp.where(member, 1.0, 0.0).astype(BF16), vectors, preferred_element_type=F32
        )

    @pl.when(step == 0)
    def _():
        acc[...] = jnp.zeros_like(acc)
        fresh = label_part()
        lv_ref[...] = fresh
        before[...] = fresh

    @pl.when(jnp.logical_and(step > 0, step < last))
    def _():
        fresh = label_part()
        acc[...] += sums_part()
        lv_ref[...] = fresh
        before[...] = fresh

    @pl.when(step == last)
    def _():
        total = acc[...] + sums_part()
        half = sub_total // 2
        own_ref[...] = total[:half].astype(BF16)
        other_ref[...] = total[half:].astype(BF16)


def label_pass(counts, rows, sub, width, sub_total):
    lab_dev, row_total = counts.shape
    tile = 512
    tiles = lab_dev // tile
    half = sub_total // 2

    def now(i):
        return (jnp.minimum(i, tiles - 1), 0)

    return pl.pallas_call(
        label_kernel,
        grid=(tiles + 1,),
        in_specs=[
            pl.BlockSpec((tile, row_total), now),
            whole(rows.shape),
            pl.BlockSpec((1, 1, tile), lambda i: (jnp.maximum(i - 1, 0), 0, 0)),
        ],
        out_specs=[pl.BlockSpec((tile, width), now), whole((half, width)), whole((half, width))],
        out_shape=[
            jax.ShapeDtypeStruct((lab_dev, width), BF16),
            jax.ShapeDtypeStruct((half, width), BF16),
            jax.ShapeDtypeStruct((half, width), BF16),
        ],
        scratch_shapes=[pltpu.VMEM((sub_total, width), F32), pltpu.VMEM((tile, width), BF16)],
        compiler_params=params(),
        cost_estimate=pl.CostEstimate(
            flops=2 * lab_dev * width * (row_total + sub_total),
            bytes_accessed=2 * lab_dev * (row_total + width),
            transcendentals=0,
        ),
        name="label_pass",
    )(counts, rows, sub.reshape(tiles, 1, tile))


def first_kernel(seed_ref, lv_ref, ids_ref, out_ref, acc, start):
    step = pl.program_id(0)

    @pl.when(step == 0)
    def _():
        acc[...] = jnp.zeros_like(acc)
        vectors = seed_ref[...].astype(BF16).astype(F32)
        start[...] = rms_rows(vectors).astype(BF16)

    vectors = lv_ref[...]
    acc[...] += jnp.dot(
        weight_rows(start[...], vectors, ids_ref[0]), vectors, preferred_element_type=F32
    )

    @pl.when(step == pl.num_programs(0) - 1)
    def _():
        out_ref[...] = acc[...].astype(BF16)


def first_pass(seeds, vectors, ids, coarse):
    lab_dev, width = vectors.shape
    tile = 1024
    tiles = lab_dev // tile
    return pl.pallas_call(
        first_kernel,
        grid=(tiles,),
        in_specs=[
            whole(seeds.shape),
            pl.BlockSpec((tile, width), lambda i: (i, 0)),
            pl.BlockSpec((1, 1, tile), lambda i: (i, 0, 0)),
        ],
        out_specs=whole((coarse, width)),
        out_shape=jax.ShapeDtypeStruct((coarse, width), BF16),
        scratch_shapes=[pltpu.VMEM((coarse, width), F32), pltpu.VMEM((coarse, width), BF16)],
        compiler_params=params(),
        cost_estimate=pl.CostEstimate(
            flops=4 * coarse * lab_dev * width, bytes_accessed=2 * lab_dev * width, transcendentals=0
        ),
        name="first_pass",
    )(seeds, vectors, ids.reshape(tiles, 1, tile))


def second_kernel(mine_ref, theirs_ref, lv_ref, ids_ref, out_ref, acc, cent):
    step = pl.program_id(0)

    @pl.when(step == 0)
    def _():
        acc[...] = jnp.zeros_like(acc)
        total = mine_ref[...].astype(F32) + theirs_ref[...].astype(F32)
        cent[...] = rms_rows(total).astype(BF16)

    vectors = lv_ref[...]
    acc[...] += jnp.dot(
        weight_rows(cent[...], vectors, ids_ref[0]), vectors, preferred_element_type=F32
    )

    @pl.when(step == pl.num_programs(0) - 1)
    def _():
        piece = out_ref.shape[2]
        per_row = acc.shape[1] // piece
        for place in range(out_ref.shape[0]):
            row, col = place // per_row, place % per_row * piece
            out_ref[place] = acc[row : row + 1, col : col + piece]


def second_pass(mine, theirs, vectors, ids, shape):
    lab_dev, width = vectors.shape
    coarse = mine.shape[0]
    tile = 1024
    tiles = lab_dev // tile
    return pl.pallas_call(
        second_kernel,
        grid=(tiles,),
        in_specs=[
            whole((coarse, width)),
            whole((coarse, width)),
            pl.BlockSpec((tile, width), lambda i: (i, 0)),
            pl.BlockSpec((1, 1, tile), lambda i: (i, 0, 0)),
        ],
        out_specs=whole(shape),
        out_shape=jax.ShapeDtypeStruct(shape, F32),
        scratch_shapes=[pltpu.VMEM((coarse, width), F32), pltpu.VMEM((coarse, width), BF16)],
        compiler_params=params(),
        cost_estimate=pl.CostEstimate(
            flops=4 * coarse * lab_dev * width, bytes_accessed=2 * lab_dev * width, transcendentals=0
        ),
        name="second_pass",
    )(mine, theirs, vectors, ids.reshape(tiles, 1, tile))


def pass_kernel(cent_total, lv_ref, ids_ref, *rest):
    cents, outs, acc = rest[:cent_total], rest[cent_total:-1], rest[-1]
    step = pl.program_id(0)

    @pl.when(step == 0)
    def _():
        acc[...] = jnp.zeros_like(acc)

    vectors = lv_ref[...]
    centroids = jnp.concatenate([cent[...] for cent in cents], axis=0)
    acc[...] += jnp.dot(
        weight_rows(centroids, vectors, ids_ref[0]), vectors, preferred_element_type=F32
    )

    @pl.when(step == pl.num_programs(0) - 1)
    def _():
        each = acc.shape[0] // len(outs)
        for index, out in enumerate(outs):
            out[...] = acc[index * each : (index + 1) * each].astype(out.dtype)


def weighted_sums(centroids, vectors, ids, outs, kind, name):
    lab_dev, width = vectors.shape
    each = centroids[0].shape[0]
    total = each * len(centroids)
    share = total // outs
    tile = 1024
    tiles = lab_dev // tile
    return pl.pallas_call(
        functools.partial(pass_kernel, len(centroids)),
        grid=(tiles,),
        in_specs=[
            pl.BlockSpec((tile, width), lambda i: (i, 0)),
            pl.BlockSpec((1, 1, tile), lambda i: (i, 0, 0)),
        ]
        + [whole((each, width))] * len(centroids),
        out_specs=[whole((share, width))] * outs,
        out_shape=[jax.ShapeDtypeStruct((share, width), kind)] * outs,
        scratch_shapes=[pltpu.VMEM((total, width), F32)],
        compiler_params=params(),
        cost_estimate=pl.CostEstimate(
            flops=4 * total * lab_dev * width, bytes_accessed=2 * lab_dev * width, transcendentals=0
        ),
        name=name,
    )(vectors, ids.reshape(tiles, 1, tile), *centroids)


def to_all(blocks):
    return lax.all_to_all(blocks, "wide", split_axis=0, concat_axis=0, tiled=True)


def to_chips(blocks):
    n = lax.axis_size("wide")
    groups = [list(range(core, n, 2)) for core in range(2)]
    return lax.all_to_all(
        blocks, "wide", split_axis=0, concat_axis=0, axis_index_groups=groups, tiled=True
    )


def core_swap(value):
    n = lax.axis_size("wide")
    return lax.ppermute(value, "wide", [(i, i ^ 1) for i in range(n)])


def spread(piece, n_wide):
    return jnp.broadcast_to(piece[None], (n_wide,) + piece.shape)


def grp_shift(value, step):
    n = lax.axis_size("grp")
    return lax.ppermute(value, "grp", [(i, (i + step) % n) for i in range(n)])


def total_of(own, others):
    own, first, second, third = (value.astype(F32) for value in (own, *others))
    return (own + second) + (first + third)


def grp_sum(value):
    return total_of(value, [grp_shift(value, step) for step in (1, 2, 3)])


def grp_gather(value):
    n = lax.axis_size("grp")
    return [value] + [grp_shift(value, n - step) for step in range(1, n)]


def grp_scatter(blocks):
    return total_of(blocks[0], [grp_shift(blocks[step], step) for step in (1, 2, 3)])


def halves(value):
    high = lax.reduce_precision(value, 8, 7)
    return high.astype(BF16), (value - high).astype(BF16)


def shards(inst_rows, inst_labels, seed_labels, coarse_first, coarse_second, sub_assign, group_map):
    n_wide = lax.axis_size("wide")
    n_grp = lax.axis_size("grp")
    lab_dev = coarse_first.shape[0]
    row_total, width = inst_rows.shape
    slots = inst_labels.shape[1]
    coarse = group_map.shape[0]
    per_dest = row_total // n_wide
    piece = coarse * width // n_wide
    me_grp = lax.axis_index("grp")
    lanes = LANES
    chunk_m = piece // lanes

    sent = sender(inst_labels.T, inst_rows, seed_labels[None], per_dest, lab_dev)
    received = to_all(sent.reshape(n_wide, per_dest // 2, 2 * width + lanes))
    beside = received[:, :, 2 * width :].astype(F32)
    received = received.reshape(row_total // 2, 2 * width + lanes)
    seed_piece = jnp.sum(beside, axis=0)[:, :PIECE]
    each = piece // PIECE
    seed_piece = (seed_piece[:each] + seed_piece[each : 2 * each]).reshape(1, piece)
    seed_piece = grp_sum(seed_piece)
    counts = label_counts(received, slots, lab_dev)
    seed_piece, _ = lax.optimization_barrier((seed_piece, counts))
    theirs = core_swap(seed_piece)
    mine_first = lax.rem(lax.axis_index("wide"), 2) == 0
    seed_row = jnp.concatenate(
        [jnp.where(mine_first, seed_piece, theirs), jnp.where(mine_first, theirs, seed_piece)],
        axis=1,
    )
    seed_sums = to_chips(spread(seed_row, n_wide // 2))

    me_core = lax.rem(lax.axis_index("wide"), 2)
    second = coarse_second.reshape(lab_dev)
    sub_total = coarse * SUB
    share = SUB // 2 // n_grp
    each = coarse * share
    core_turn = (sub_assign // (SUB // 2)) ^ me_core
    grp_turn = lax.rem(sub_assign // share + (n_grp - me_grp), n_grp)
    sub_ids = (core_turn * n_grp + grp_turn) * each + second * share + sub_assign % share
    label_vectors, own_half, other_half = label_pass(counts, received, sub_ids, width, sub_total)

    def reduced(own, other, *more):
        half = (own.astype(F32) + core_swap(other).astype(F32)).astype(BF16)
        return grp_scatter(
            [jnp.concatenate([half[i * each : (i + 1) * each], *more]) for i in range(n_grp)]
        )

    m_one = first_pass(rms_rows(seed_sums.reshape(coarse, width)), label_vectors, coarse_first, coarse)
    parts = reduced(own_half, other_half, m_one).astype(BF16)
    sub_mine, m_one = parts[:each], parts[each:]
    chips = n_wide // 2
    sent = jnp.concatenate(
        [sub_mine.reshape(chips, share, width), m_one.reshape(chips, share, piece)], axis=2
    )
    got = jnp.sum(to_chips(sent).astype(F32), axis=0)

    sent = jnp.concatenate([rms_rows(got[:, :width]), got[:, width:]], axis=1).astype(BF16)
    got = to_chips(spread(sent, chips))
    first = got[:, :, width:].reshape(coarse, width)
    sub_own = got[:, :, :width].reshape(each, width)

    theirs, sub_own = lax.optimization_barrier((core_swap(first), sub_own))
    m_two = second_pass(first, theirs, label_vectors, second, (n_wide, 1, piece))
    two_parts = to_all(m_two).reshape(n_wide, piece)

    sub_start = grp_gather(sub_own)
    _, *sub_start = lax.optimization_barrier((m_two, *sub_start))
    sub_start = sub_start + [core_swap(block) for block in sub_start]
    w_own, w_other = weighted_sums(sub_start, label_vectors, sub_ids, 2, BF16, "sub_pass")
    high, low = halves(jnp.sum(two_parts, axis=0))
    two_row = jnp.concatenate([high, low])[None]
    w_mine = reduced(w_own, w_other, jnp.pad(two_row, ((0, 7), (0, 0))))
    two_piece = w_mine[each, :piece] + w_mine[each, piece:]
    w_mine = w_mine[:each].astype(BF16)
    host = (
        group_map[None, :] == lax.broadcasted_iota(jnp.int32, (n_wide, coarse), 0)
    ).astype(BF16)
    to_hosts = jnp.dot(
        host, w_mine.reshape(coarse, share * width), preferred_element_type=F32
    ).astype(BF16)
    two_piece = jnp.stack(halves(two_piece))
    sent = jnp.concatenate(
        [to_hosts.reshape(n_wide, share, width), spread(two_piece, n_wide)], axis=2
    )
    got = to_all(sent).astype(F32)
    hosted = jnp.sum(got[:, :, :width].reshape(chips, 2, share, width), axis=0)
    hosted = rms_rows(hosted.reshape(2 * share, width))
    last = got[:, 0, width:] + got[:, 1, width:]
    coarse_centroids = rms_rows(last.reshape(coarse, width))
    pieces = grp_gather(hosted)
    ordered = []
    for position in range(n_grp):
        turn = lax.rem(position + (n_grp - me_grp), n_grp)
        value = pieces[0]
        for index in range(1, n_grp):
            value = jnp.where(turn == index, pieces[index], value)
        ordered.append(value.reshape(2, 1, share, width))
    sub_centroids = jnp.concatenate(ordered, axis=1).reshape(1, SUB, width)
    return label_vectors, coarse_centroids, sub_centroids


def solution(mesh):
    in_specs = (
        P(("wide", "grp"), None),
        P(("wide", "grp"), None),
        P(),
        P(("wide", "grp")),
        P(("wide", "grp"), None),
        P(("wide", "grp")),
        P(),
    )
    out_specs = (P(("wide", "grp"), None), P(), P("wide", None, None))
    return jax.shard_map(shards, mesh=mesh, in_specs=in_specs, out_specs=out_specs, check_vma=False)
```

```python
import functools

import jax
import jax.numpy as jnp
from jax import lax
from jax.experimental import pallas as pl
from jax.experimental.pallas import tpu as pltpu
from jax.sharding import PartitionSpec as P

SUB = 16
EPSILON = 1e-06
CONCENTRATION = 16.0
TILE = 512
LANES = 128
PIECE = 96
VMEM_LIMIT = 56 * 1024 * 1024

F32 = jnp.float32
BF16 = jnp.bfloat16


def rms_rows(matrix):
    return matrix * lax.rsqrt(jnp.mean(matrix * matrix, axis=-1, keepdims=True) + EPSILON)


def params():
    return pltpu.CompilerParams(
        dimension_semantics=("arbitrary",), vmem_limit_bytes=VMEM_LIMIT
    )


def whole(shape):
    return pl.BlockSpec(shape, lambda i: (0,) * len(shape))


def halved(rows, per_dest):
    total, width = rows.shape
    half = per_dest // 2
    parts = rows.astype(F32).reshape(total // per_dest, 2, half, width)
    return [parts[:, i].reshape(total // 2, width) for i in range(2)]


def sender_kernel(per_dest, lab_dev, labels_ref, rows_ref, seeds_ref, out_ref):
    slots, row_total = labels_ref.shape
    width = rows_ref.shape[1]
    coarse = seeds_ref.shape[1]
    labels = labels_ref[...]
    diagonal = lax.broadcasted_iota(jnp.int32, (coarse, coarse), 0)
    diagonal = diagonal == lax.broadcasted_iota(jnp.int32, (coarse, coarse), 1)
    seeds = jnp.where(diagonal, seeds_ref[...].astype(F32), 0.0)
    seeds = jnp.sum(seeds, axis=1, keepdims=True).astype(jnp.int32)
    block = lax.broadcasted_iota(jnp.int32, (coarse, row_total), 1) // per_dest
    owner = block * lax.axis_size("grp") + lax.axis_index("grp")
    wanted = seeds - owner * lab_dev
    counts = jnp.zeros((coarse, row_total), F32)
    for slot in range(slots):
        counts = counts + jnp.where(labels[slot : slot + 1, :] == wanted, 1.0, 0.0)
    part = jnp.dot(counts.astype(BF16), rows_ref[...], preferred_element_type=F32)
    high = part.astype(BF16)
    low = (part - high.astype(F32)).astype(BF16)
    filler = jnp.zeros((coarse, LANES - PIECE), BF16)
    pieces = width // PIECE
    table = []
    for value in (high, low):
        for index in range(pieces):
            chunk = value[:, index * PIECE : (index + 1) * PIECE]
            table.append(jnp.concatenate([chunk, filler], axis=1))
    table = jnp.concatenate(table, axis=0)
    half = per_dest // 2
    row = lax.broadcasted_iota(jnp.int32, (row_total // 2, 1), 0)
    dest, place = row // half, row % half
    each = pieces // 2
    index = (place // each * pieces + dest % 2 * each + place % each) * coarse + dest // 2
    picked = lax.broadcasted_iota(jnp.int32, (row_total // 2, table.shape[0]), 1) == index
    beside = jnp.dot(
        jnp.where(picked, 1.0, 0.0).astype(BF16), table, preferred_element_type=F32
    )
    digits = jnp.concatenate([labels // 256, labels % 256], axis=0).astype(F32)
    shape = (2 * slots, LANES)
    for index, part in enumerate(halved(digits.T, per_dest)):
        shift = lax.broadcasted_iota(jnp.int32, shape, 0) + PIECE + index * 2 * slots
        shift = shift == lax.broadcasted_iota(jnp.int32, shape, 1)
        beside = beside + jnp.dot(
            part.astype(BF16),
            jnp.where(shift, 1.0, 0.0).astype(BF16),
            preferred_element_type=F32,
        )
    for index, part in enumerate(halved(rows_ref[...], per_dest)):
        out_ref[:, index * width : (index + 1) * width] = part.astype(BF16)
    out_ref[:, 2 * width :] = beside.astype(BF16)


def sender(labels, rows, seeds, per_dest, lab_dev):
    row_total, width = rows.shape
    shape = (row_total // 2, 2 * width + LANES)
    return pl.pallas_call(
        functools.partial(sender_kernel, per_dest, lab_dev),
        grid=(1,),
        in_specs=[whole(labels.shape), whole(rows.shape), whole(seeds.shape)],
        out_specs=whole(shape),
        out_shape=jax.ShapeDtypeStruct(shape, BF16),
        compiler_params=params(),
        name="sender",
    )(labels, rows, seeds)


def counts_kernel(beside_ref, out_ref, labels_ref):
    shape = out_ref.shape
    slots = labels_ref.shape[0]

    @pl.when(pl.program_id(0) == 0)
    def _():
        turned = beside_ref[...].astype(F32).T
        half = turned.shape[1]
        for index in range(2):
            first = PIECE + index * 2 * slots
            labels = turned[first : first + slots] * 256.0
            labels = labels + turned[first + slots : first + 2 * slots]
            labels_ref[:, index * half : (index + 1) * half] = labels.astype(jnp.int32)

    labels = (labels_ref[...] - pl.program_id(0) * shape[0]).astype(jnp.int16)
    label = lax.broadcasted_iota(jnp.int32, shape, 0).astype(jnp.int16)
    one, zero = jnp.ones((), BF16), jnp.zeros((), BF16)
    total = jnp.zeros(shape, BF16)
    for slot in range(slots):
        named = jnp.broadcast_to(labels[slot : slot + 1, :], shape)
        total = total + jnp.where(named == label, one, zero)
    out_ref[...] = total


def label_counts(received, slots, lab_dev):
    half, full = received.shape
    rows = 2 * half
    return pl.pallas_call(
        counts_kernel,
        grid=(lab_dev // TILE,),
        in_specs=[pl.BlockSpec((half, LANES), lambda i: (0, full // LANES - 1))],
        out_specs=pl.BlockSpec((TILE, rows), lambda i: (i, 0)),
        out_shape=jax.ShapeDtypeStruct((lab_dev, rows), BF16),
        scratch_shapes=[pltpu.VMEM((slots, rows), jnp.int32)],
        compiler_params=params(),
        cost_estimate=pl.CostEstimate(
            flops=3 * slots * rows * lab_dev, bytes_accessed=2 * rows * lab_dev, transcendentals=0
        ),
        name="label_counts",
    )(received)


def weight_rows(centroids, vectors, ids_row):
    scores = lax.dot_general(
        centroids, vectors, (((1,), (1,)), ((), ())), preferred_element_type=F32
    )
    member = ids_row == lax.broadcasted_iota(jnp.int32, scores.shape, 0)
    cosine = jnp.sum(jnp.where(member, scores, 0.0), axis=0, keepdims=True) / vectors.shape[1]
    weight = jnp.exp(CONCENTRATION * cosine)
    return jnp.where(member, weight, 0.0).astype(BF16)


def label_kernel(
    counts_ref, rows_ref, sub_ref, lv_ref, own_ref, other_ref, acc, before
):
    step, last = pl.program_id(0), pl.num_programs(0) - 1
    sub_total, width = acc.shape

    def label_part():
        half = rows_ref.shape[0]
        sums = jnp.dot(counts_ref[:, :half], rows_ref[:, :width], preferred_element_type=F32)
        sums = sums + jnp.dot(
            counts_ref[:, half:], rows_ref[:, width : 2 * width], preferred_element_type=F32
        )
        return rms_rows(sums).astype(BF16)

    def sums_part():
        vectors = before[...]
        member = sub_ref[0] == lax.broadcasted_iota(jnp.int32, (sub_total, vectors.shape[0]), 0)
        return jnp.dot(
            jnp.where(member, 1.0, 0.0).astype(BF16), vectors, preferred_element_type=F32
        )

    @pl.when(step == 0)
    def _():
        acc[...] = jnp.zeros_like(acc)
        fresh = label_part()
        lv_ref[...] = fresh
        before[...] = fresh

    @pl.when(jnp.logical_and(step > 0, step < last))
    def _():
        fresh = label_part()
        acc[...] += sums_part()
        lv_ref[...] = fresh
        before[...] = fresh

    @pl.when(step == last)
    def _():
        total = acc[...] + sums_part()
        half = sub_total // 2
        own_ref[...] = total[:half].astype(BF16)
        other_ref[...] = total[half:].astype(BF16)


def label_pass(counts, rows, sub, width, sub_total):
    lab_dev, row_total = counts.shape
    tile = 512
    tiles = lab_dev // tile
    half = sub_total // 2

    def now(i):
        return (jnp.minimum(i, tiles - 1), 0)

    return pl.pallas_call(
        label_kernel,
        grid=(tiles + 1,),
        in_specs=[
            pl.BlockSpec((tile, row_total), now),
            whole(rows.shape),
            pl.BlockSpec((1, 1, tile), lambda i: (jnp.maximum(i - 1, 0), 0, 0)),
        ],
        out_specs=[pl.BlockSpec((tile, width), now), whole((half, width)), whole((half, width))],
        out_shape=[
            jax.ShapeDtypeStruct((lab_dev, width), BF16),
            jax.ShapeDtypeStruct((half, width), BF16),
            jax.ShapeDtypeStruct((half, width), BF16),
        ],
        scratch_shapes=[pltpu.VMEM((sub_total, width), F32), pltpu.VMEM((tile, width), BF16)],
        compiler_params=params(),
        cost_estimate=pl.CostEstimate(
            flops=2 * lab_dev * width * (row_total + sub_total),
            bytes_accessed=2 * lab_dev * (row_total + width),
            transcendentals=0,
        ),
        name="label_pass",
    )(counts, rows, sub.reshape(tiles, 1, tile))


def first_kernel(seed_ref, lv_ref, ids_ref, out_ref, acc, start):
    step = pl.program_id(0)

    @pl.when(step == 0)
    def _():
        acc[...] = jnp.zeros_like(acc)
        vectors = seed_ref[...].astype(BF16).astype(F32)
        start[...] = rms_rows(vectors).astype(BF16)

    vectors = lv_ref[...]
    acc[...] += jnp.dot(
        weight_rows(start[...], vectors, ids_ref[0]), vectors, preferred_element_type=F32
    )

    @pl.when(step == pl.num_programs(0) - 1)
    def _():
        out_ref[...] = acc[...].astype(BF16)


def first_pass(seeds, vectors, ids, coarse):
    lab_dev, width = vectors.shape
    tile = 1024
    tiles = lab_dev // tile
    return pl.pallas_call(
        first_kernel,
        grid=(tiles,),
        in_specs=[
            whole(seeds.shape),
            pl.BlockSpec((tile, width), lambda i: (i, 0)),
            pl.BlockSpec((1, 1, tile), lambda i: (i, 0, 0)),
        ],
        out_specs=whole((coarse, width)),
        out_shape=jax.ShapeDtypeStruct((coarse, width), BF16),
        scratch_shapes=[pltpu.VMEM((coarse, width), F32), pltpu.VMEM((coarse, width), BF16)],
        compiler_params=params(),
        cost_estimate=pl.CostEstimate(
            flops=4 * coarse * lab_dev * width, bytes_accessed=2 * lab_dev * width, transcendentals=0
        ),
        name="first_pass",
    )(seeds, vectors, ids.reshape(tiles, 1, tile))


def second_kernel(mine_ref, theirs_ref, lv_ref, ids_ref, out_ref, acc, cent):
    step = pl.program_id(0)

    @pl.when(step == 0)
    def _():
        acc[...] = jnp.zeros_like(acc)
        total = mine_ref[...].astype(F32) + theirs_ref[...].astype(F32)
        cent[...] = rms_rows(total).astype(BF16)

    vectors = lv_ref[...]
    acc[...] += jnp.dot(
        weight_rows(cent[...], vectors, ids_ref[0]), vectors, preferred_element_type=F32
    )

    @pl.when(step == pl.num_programs(0) - 1)
    def _():
        piece = out_ref.shape[2]
        per_row = acc.shape[1] // piece
        for place in range(out_ref.shape[0]):
            row, col = place // per_row, place % per_row * piece
            out_ref[place] = acc[row : row + 1, col : col + piece]


def second_pass(mine, theirs, vectors, ids, shape):
    lab_dev, width = vectors.shape
    coarse = mine.shape[0]
    tile = 1024
    tiles = lab_dev // tile
    return pl.pallas_call(
        second_kernel,
        grid=(tiles,),
        in_specs=[
            whole((coarse, width)),
            whole((coarse, width)),
            pl.BlockSpec((tile, width), lambda i: (i, 0)),
            pl.BlockSpec((1, 1, tile), lambda i: (i, 0, 0)),
        ],
        out_specs=whole(shape),
        out_shape=jax.ShapeDtypeStruct(shape, F32),
        scratch_shapes=[pltpu.VMEM((coarse, width), F32), pltpu.VMEM((coarse, width), BF16)],
        compiler_params=params(),
        cost_estimate=pl.CostEstimate(
            flops=4 * coarse * lab_dev * width, bytes_accessed=2 * lab_dev * width, transcendentals=0
        ),
        name="second_pass",
    )(mine, theirs, vectors, ids.reshape(tiles, 1, tile))


def pass_kernel(cent_total, lv_ref, ids_ref, *rest):
    cents, outs, acc = rest[:cent_total], rest[cent_total:-1], rest[-1]
    step = pl.program_id(0)

    @pl.when(step == 0)
    def _():
        acc[...] = jnp.zeros_like(acc)

    vectors = lv_ref[...]
    centroids = jnp.concatenate([cent[...] for cent in cents], axis=0)
    acc[...] += jnp.dot(
        weight_rows(centroids, vectors, ids_ref[0]), vectors, preferred_element_type=F32
    )

    @pl.when(step == pl.num_programs(0) - 1)
    def _():
        each = acc.shape[0] // len(outs)
        for index, out in enumerate(outs):
            out[...] = acc[index * each : (index + 1) * each].astype(out.dtype)


def weighted_sums(centroids, vectors, ids, outs, kind, name):
    lab_dev, width = vectors.shape
    each = centroids[0].shape[0]
    total = each * len(centroids)
    share = total // outs
    tile = 1024
    tiles = lab_dev // tile
    return pl.pallas_call(
        functools.partial(pass_kernel, len(centroids)),
        grid=(tiles,),
        in_specs=[
            pl.BlockSpec((tile, width), lambda i: (i, 0)),
            pl.BlockSpec((1, 1, tile), lambda i: (i, 0, 0)),
        ]
        + [whole((each, width))] * len(centroids),
        out_specs=[whole((share, width))] * outs,
        out_shape=[jax.ShapeDtypeStruct((share, width), kind)] * outs,
        scratch_shapes=[pltpu.VMEM((total, width), F32)],
        compiler_params=params(),
        cost_estimate=pl.CostEstimate(
            flops=4 * total * lab_dev * width, bytes_accessed=2 * lab_dev * width, transcendentals=0
        ),
        name=name,
    )(vectors, ids.reshape(tiles, 1, tile), *centroids)


def to_all(blocks):
    return lax.all_to_all(blocks, "wide", split_axis=0, concat_axis=0, tiled=True)


def to_chips(blocks):
    n = lax.axis_size("wide")
    groups = [list(range(core, n, 2)) for core in range(2)]
    return lax.all_to_all(
        blocks, "wide", split_axis=0, concat_axis=0, axis_index_groups=groups, tiled=True
    )


def core_swap(value):
    n = lax.axis_size("wide")
    return lax.ppermute(value, "wide", [(i, i ^ 1) for i in range(n)])


def spread(piece, n_wide):
    return jnp.broadcast_to(piece[None], (n_wide,) + piece.shape)


def grp_shift(value, step):
    n = lax.axis_size("grp")
    return lax.ppermute(value, "grp", [(i, (i + step) % n) for i in range(n)])


def total_of(own, others):
    own, first, second, third = (value.astype(F32) for value in (own, *others))
    return (own + second) + (first + third)


def grp_sum(value):
    return total_of(value, [grp_shift(value, step) for step in (1, 2, 3)])


def grp_gather(value):
    n = lax.axis_size("grp")
    return [value] + [grp_shift(value, n - step) for step in range(1, n)]


def grp_scatter(blocks):
    return total_of(blocks[0], [grp_shift(blocks[step], step) for step in (1, 2, 3)])


def halves(value):
    high = lax.reduce_precision(value, 8, 7)
    return high.astype(BF16), (value - high).astype(BF16)


def shards(inst_rows, inst_labels, seed_labels, coarse_first, coarse_second, sub_assign, group_map):
    n_wide = lax.axis_size("wide")
    n_grp = lax.axis_size("grp")
    lab_dev = coarse_first.shape[0]
    row_total, width = inst_rows.shape
    slots = inst_labels.shape[1]
    coarse = group_map.shape[0]
    per_dest = row_total // n_wide
    piece = coarse * width // n_wide
    me_grp = lax.axis_index("grp")
    lanes = LANES
    chunk_m = piece // lanes

    sent = sender(inst_labels.T, inst_rows, seed_labels[None], per_dest, lab_dev)
    received = to_all(sent.reshape(n_wide, per_dest // 2, 2 * width + lanes))
    beside = received[:, :, 2 * width :].astype(F32)
    received = received.reshape(row_total // 2, 2 * width + lanes)
    seed_piece = jnp.sum(beside, axis=0)[:, :PIECE]
    each = piece // PIECE
    seed_piece = (seed_piece[:each] + seed_piece[each : 2 * each]).reshape(1, piece)
    seed_piece = grp_sum(seed_piece)
    counts = label_counts(received, slots, lab_dev)
    seed_piece, _ = lax.optimization_barrier((seed_piece, counts))
    theirs = core_swap(seed_piece)
    mine_first = lax.rem(lax.axis_index("wide"), 2) == 0
    seed_row = jnp.concatenate(
        [jnp.where(mine_first, seed_piece, theirs), jnp.where(mine_first, theirs, seed_piece)],
        axis=1,
    )
    seed_sums = to_chips(spread(seed_row, n_wide // 2))

    me_core = lax.rem(lax.axis_index("wide"), 2)
    second = coarse_second.reshape(lab_dev)
    sub_total = coarse * SUB
    share = SUB // 2 // n_grp
    each = coarse * share
    core_turn = (sub_assign // (SUB // 2)) ^ me_core
    grp_turn = lax.rem(sub_assign // share + (n_grp - me_grp), n_grp)
    sub_ids = (core_turn * n_grp + grp_turn) * each + second * share + sub_assign % share
    label_vectors, own_half, other_half = label_pass(counts, received, sub_ids, width, sub_total)

    def reduced(own, other, *more):
        half = (own.astype(F32) + core_swap(other).astype(F32)).astype(BF16)
        return grp_scatter(
            [jnp.concatenate([half[i * each : (i + 1) * each], *more]) for i in range(n_grp)]
        )

    m_one = first_pass(rms_rows(seed_sums.reshape(coarse, width)), label_vectors, coarse_first, coarse)
    parts = reduced(own_half, other_half, m_one).astype(BF16)
    sub_mine, m_one = parts[:each], parts[each:]
    chips = n_wide // 2
    sent = jnp.concatenate(
        [sub_mine.reshape(chips, share, width), m_one.reshape(chips, share, piece)], axis=2
    )
    got = jnp.sum(to_chips(sent).astype(F32), axis=0)

    sent = jnp.concatenate([rms_rows(got[:, :width]), got[:, width:]], axis=1).astype(BF16)
    got = to_chips(spread(sent, chips))
    first = got[:, :, width:].reshape(coarse, width)
    sub_own = got[:, :, :width].reshape(each, width)

    theirs, sub_own = lax.optimization_barrier((core_swap(first), sub_own))
    m_two = second_pass(first, theirs, label_vectors, second, (chips, 1, width))
    two_parts = to_chips(m_two).reshape(chips, width)

    sub_start = grp_gather(sub_own)
    _, *sub_start = lax.optimization_barrier((m_two, *sub_start))
    sub_start = sub_start + [core_swap(block) for block in sub_start]
    w_own, w_other = weighted_sums(sub_start, label_vectors, sub_ids, 2, BF16, "sub_pass")
    two_sum = jnp.sum(two_parts, axis=0)
    two_sum = two_sum + core_swap(two_sum)
    high, low = halves(jnp.where(me_core == 0, two_sum[:piece], two_sum[piece:]))
    two_row = jnp.concatenate([high, low])[None]
    w_mine = reduced(w_own, w_other, jnp.pad(two_row, ((0, 7), (0, 0))))
    two_piece = w_mine[each, :piece] + w_mine[each, piece:]
    w_mine = w_mine[:each].astype(BF16)
    host = (
        group_map[None, :] == lax.broadcasted_iota(jnp.int32, (n_wide, coarse), 0)
    ).astype(BF16)
    to_hosts = jnp.dot(
        host, w_mine.reshape(coarse, share * width), preferred_element_type=F32
    ).astype(BF16)
    two_piece = jnp.stack(halves(two_piece))
    sent = jnp.concatenate(
        [to_hosts.reshape(n_wide, share, width), spread(two_piece, n_wide)], axis=2
    )
    got = to_all(sent).astype(F32)
    hosted = jnp.sum(got[:, :, :width].reshape(chips, 2, share, width), axis=0)
    hosted = rms_rows(hosted.reshape(2 * share, width))
    last = got[:, 0, width:] + got[:, 1, width:]
    coarse_centroids = rms_rows(last.reshape(coarse, width))
    pieces = grp_gather(hosted)
    ordered = []
    for position in range(n_grp):
        turn = lax.rem(position + (n_grp - me_grp), n_grp)
        value = pieces[0]
        for index in range(1, n_grp):
            value = jnp.where(turn == index, pieces[index], value)
        ordered.append(value.reshape(2, 1, share, width))
    sub_centroids = jnp.concatenate(ordered, axis=1).reshape(1, SUB, width)
    return label_vectors, coarse_centroids, sub_centroids


def solution(mesh):
    in_specs = (
        P(("wide", "grp"), None),
        P(("wide", "grp"), None),
        P(),
        P(("wide", "grp")),
        P(("wide", "grp"), None),
        P(("wide", "grp")),
        P(),
    )
    out_specs = (P(("wide", "grp"), None), P(), P("wide", None, None))
    return jax.shard_map(shards, mesh=mesh, in_specs=in_specs, out_specs=out_specs, check_vma=False)
```
